32 devices in a mesh: ctx: 8 (over z, x), fsdp: 4 (over y, core).
Axes of the slice: x: 2, y: 2, z: 4, core: 2. Of those that a mesh axis runs over, the one named last changes fastest.
Arguments:
- x_cur: bfloat16 [4, 2048, 2048], P('fsdp', 'ctx'), may hold values from -6 to 6
- x_next: bfloat16 [4, 2048, 2048], P('fsdp', 'ctx'), may hold values from -6 to 6
- cot_cur: bfloat16 [4, 2048, 2048], P('fsdp', 'ctx'), may hold values from -6 to 6
- cot_next: bfloat16 [4, 2048, 2048], P('fsdp', 'ctx'), may hold values from -6 to 6
- w_q: bfloat16 [2048, 1024], P('fsdp')
- w_kv: bfloat16 [2048, 512], P('fsdp')
- w_out: bfloat16 [2048, 1024], P('fsdp'), may hold values from -0.1875 to 0.1875
Outputs:
- x_prev: bfloat16 [4, 2048, 2048], P('fsdp', 'ctx')
- grad_cur: bfloat16 [4, 2048, 2048], P('fsdp', 'ctx')
- grad_weights: float32 [2048, 2560], P(('ctx', 'fsdp'))
The draws below stay inside these ranges and needn't reach their ends.
All inputs are finite; a program needn't handle non-finite values.
Results may differ from the reference program's by a relative error of at most 0.015.
The reference program's roundings to bfloat16 on the way (of `hidden`, `grad_attn`, `probs_low`, `attended`, `grad_scores`, `grad_query` and `grad_kv`) count: a program that leaves them out, or rounds other values in their place, can miss the bound.
Values may be sent and summed in bfloat16 or wider, within the bound.
A program may use at most 192 MiB of HBM per device.

```python
import math
import jax
import jax.numpy as jnp
from jax import lax

MODEL_WIDTH = 2048
QUERY_HEADS = 8
KEY_VALUE_HEADS = 2
HEAD_SIZE = 128
WINDOW_TOKENS = 1024
SHARD = 256
SEQS = 4
SEQUENCE_TOKENS = 2048


def query_start_index(key):
    unscaled_scores = jax.random.normal(jax.random.fold_in(key, 101), (MODEL_WIDTH, QUERY_HEADS * HEAD_SIZE), jnp.float32)
    return jnp.clip(unscaled_scores, -6.0, 6.0) * (1.0 / math.sqrt(MODEL_WIDTH))


def draw_w_q(key, part):
    return query_start_index(key).astype(jnp.bfloat16)


def draw_w_kv(key, part):
    unscaled_scores = jax.random.normal(jax.random.fold_in(key, 102), (MODEL_WIDTH, 2 * KEY_VALUE_HEADS * HEAD_SIZE), jnp.float32)
    unscaled_scores = jnp.clip(unscaled_scores, -6.0, 6.0) * (1.0 / math.sqrt(MODEL_WIDTH))
    return unscaled_scores.astype(jnp.bfloat16)


def levels(stream_key, dims, cuts, low, top_value):
    factor_of = 1.0
    for dim, shards_of in cuts:
        steps = jax.random.uniform(jax.random.fold_in(jax.random.fold_in(stream_key, 6), dim), (shards_of,), jnp.float32, low / len(cuts), top_value / len(cuts))
        factor_of = factor_of * jnp.repeat(jnp.exp(steps), dims[dim] // shards_of).reshape((-1,) + (1,) * (len(dims) - 1 - dim))
    return factor_of


def centred(own_key, dims, width, reach, split=(), kind=jnp.bfloat16):
    result = width * jax.random.normal(own_key, dims, jnp.float32)
    if split:
        result = result * levels(own_key, dims, split, -0.22, 0.18)
    return jnp.clip(result, -reach, reach).astype(kind)


def setup_inputs(seed: int = 0) -> dict:
    seeds = jax.random.split(jax.random.key(seed), 8)
    return {
        "x_cur": centred(seeds[0], (SEQS, SEQUENCE_TOKENS, MODEL_WIDTH), 1.0, 6.0, ((0, 4), (1, 8))),
        "x_next": centred(seeds[1], (SEQS, SEQUENCE_TOKENS, MODEL_WIDTH), 1.0, 6.0, ((0, 4), (1, 8))),
        "cot_cur": centred(seeds[2], (SEQS, SEQUENCE_TOKENS, MODEL_WIDTH), 1.0, 6.0, ((0, 4), (1, 8))),
        "cot_next": centred(seeds[3], (SEQS, SEQUENCE_TOKENS, MODEL_WIDTH), 1.0, 6.0, ((0, 4), (1, 8))),
        "w_q": draw_w_q(jax.random.fold_in(seeds[7], 71), 0),
        "w_kv": draw_w_kv(jax.random.fold_in(seeds[7], 71), 0),
        "w_out": centred(seeds[6], (MODEL_WIDTH, QUERY_HEADS * HEAD_SIZE), (QUERY_HEADS * HEAD_SIZE) ** -0.5, 0.1875, ((0, 4),)),
    }


EPS = 1e-05

def normalize(rows):
    values = rows.astype(jnp.float32)
    inv_rms = lax.rsqrt(lax.optimization_barrier(jnp.mean(values * values, axis=-1, keepdims=True)) + EPS)
    return (values * inv_rms, inv_rms)

def window_block(query_rows, key_value_pairs, output_gradient, base):
    window_extent = key_value_pairs.shape[0]
    element_count = query_rows.shape[0]
    query_group = QUERY_HEADS // KEY_VALUE_HEADS
    scale = 1.0 / math.sqrt(HEAD_SIZE)
    query_pos = base + jnp.arange(element_count, dtype=jnp.int32)
    key_pos = base - WINDOW_TOKENS + jnp.arange(window_extent, dtype=jnp.int32)
    offset = query_pos[:, None] - key_pos[None, :]
    allowed = (offset >= 0) & (offset < WINDOW_TOKENS) & (key_pos[None, :] >= 0)
    query_grouped = query_rows.reshape(element_count, KEY_VALUE_HEADS, query_group, HEAD_SIZE).astype(jnp.float32)
    key_tensor = key_value_pairs[:, :KEY_VALUE_HEADS * HEAD_SIZE].reshape(window_extent, KEY_VALUE_HEADS, HEAD_SIZE).astype(jnp.float32)
    value_tensor = key_value_pairs[:, KEY_VALUE_HEADS * HEAD_SIZE:].reshape(window_extent, KEY_VALUE_HEADS, HEAD_SIZE).astype(jnp.float32)
    scores = jnp.einsum('igmd,jgd->gmij', query_grouped, key_tensor) * scale
    scores = jnp.where(allowed[None, None], scores, -jnp.inf)
    top = lax.optimization_barrier(jnp.max(scores, axis=-1, keepdims=True))
    expo = jnp.exp(scores - top)
    probs = expo / lax.optimization_barrier(jnp.sum(expo, axis=-1, keepdims=True))
    probs_low = lax.optimization_barrier(probs.astype(jnp.bfloat16)).astype(jnp.float32)
    attended = jnp.einsum('gmij,jgd->igmd', probs_low, value_tensor)
    gradient_grouped = output_gradient.reshape(element_count, KEY_VALUE_HEADS, query_group, HEAD_SIZE).astype(jnp.float32)
    grad_probs = jnp.einsum('igmd,jgd->gmij', gradient_grouped, value_tensor)
    delta = jnp.einsum('igmd,igmd->gmi', gradient_grouped, attended)
    grad_scores = (probs * (grad_probs - delta[..., None]) * scale).astype(jnp.bfloat16)
    grad_scores = lax.optimization_barrier(grad_scores).astype(jnp.float32)
    grad_query = jnp.einsum('gmij,jgd->igmd', grad_scores, key_tensor).astype(jnp.bfloat16)
    key_gradient = jnp.einsum('gmij,igmd->jgd', grad_scores, query_grouped)
    value_gradient = jnp.einsum('gmij,igmd->jgd', probs_low, gradient_grouped)
    value_partial_sum = jnp.concatenate([key_gradient.reshape(window_extent, KEY_VALUE_HEADS * HEAD_SIZE), value_gradient.reshape(window_extent, KEY_VALUE_HEADS * HEAD_SIZE)], 1)
    return (attended.astype(jnp.bfloat16).reshape(element_count, QUERY_HEADS * HEAD_SIZE), grad_query.reshape(element_count, QUERY_HEADS * HEAD_SIZE), value_partial_sum.astype(jnp.bfloat16))

def reference(x_cur, x_next, cot_cur, cot_next, w_q, w_kv, w_out):
    contract_cols = (((1,), (1,)), ((), ()))
    contract_rows = (((0,), (0,)), ((), ()))
    window_extent = WINDOW_TOKENS + SHARD

    def one_sequence(total, items):
        x_row, next_row, cot_row, cotn_row = items
        normed, inv_rms = normalize(x_row)
        hidden = normed.astype(jnp.bfloat16)
        query_rows = jnp.dot(hidden, w_q, preferred_element_type=jnp.float32).astype(jnp.bfloat16)
        key_value_pairs = jnp.dot(hidden, w_kv, preferred_element_type=jnp.float32).astype(jnp.bfloat16)
        grad_attn = (2.0 * jnp.dot(cotn_row, w_out, preferred_element_type=jnp.float32)).astype(jnp.bfloat16)
        padded_input = jnp.concatenate([jnp.zeros((WINDOW_TOKENS, 2 * KEY_VALUE_HEADS * HEAD_SIZE), key_value_pairs.dtype), key_value_pairs], 0)

        def one_block(accum, index):
            start = (index * SHARD).astype(jnp.int32)
            q_block = lax.dynamic_slice_in_dim(query_rows, start, SHARD, 0)
            kv_block = lax.dynamic_slice_in_dim(padded_input, start, window_extent, 0)
            g_block = lax.dynamic_slice_in_dim(grad_attn, start, SHARD, 0)
            out_block, dq_block, value_partial_sum = window_block(q_block, kv_block, g_block, start)
            current = lax.dynamic_slice_in_dim(accum, start, window_extent, 0)
            accum = lax.dynamic_update_slice_in_dim(accum, current + value_partial_sum.astype(jnp.float32), start, 0)
            return (accum, (out_block, dq_block))
        initial_accumulator = jnp.zeros((WINDOW_TOKENS + SEQUENCE_TOKENS, 2 * KEY_VALUE_HEADS * HEAD_SIZE), jnp.float32)
        accum, (out_blocks, dq_blocks) = lax.scan(one_block, initial_accumulator, jnp.arange(SEQUENCE_TOKENS // SHARD, dtype=jnp.int32))
        attended = out_blocks.reshape(SEQUENCE_TOKENS, QUERY_HEADS * HEAD_SIZE)
        grad_query = dq_blocks.reshape(SEQUENCE_TOKENS, QUERY_HEADS * HEAD_SIZE)
        grad_kv = accum[WINDOW_TOKENS:].astype(jnp.bfloat16)
        layer_out = lax.dot_general(attended, w_out, contract_cols, preferred_element_type=jnp.float32)
        prev_row = (next_row.astype(jnp.float32) - 2.0 * layer_out).astype(jnp.bfloat16)
        grad_hidden = lax.dot_general(grad_query, w_q, contract_cols, preferred_element_type=jnp.float32)
        grad_hidden = grad_hidden + lax.dot_general(grad_kv, w_kv, contract_cols, preferred_element_type=jnp.float32)
        grad_x = inv_rms * (grad_hidden - normed * lax.optimization_barrier(jnp.mean(grad_hidden * normed, axis=-1, keepdims=True)))
        grad_row = (cot_row.astype(jnp.float32) + grad_x).astype(jnp.bfloat16)
        left = jnp.concatenate([grad_query, grad_kv], 1)
        term_in = lax.dot_general(hidden, left, contract_rows, preferred_element_type=jnp.float32)
        term_out = 2.0 * lax.dot_general(cotn_row, attended, contract_rows, preferred_element_type=jnp.float32)
        total = total + jnp.concatenate([term_in, term_out], 1)
        return (total, (prev_row, grad_row))
    initial_total = jnp.zeros((MODEL_WIDTH, 2 * QUERY_HEADS * HEAD_SIZE + 2 * KEY_VALUE_HEADS * HEAD_SIZE), jnp.float32)
    total, (x_prev, grad_cur) = lax.scan(one_sequence, initial_total, (x_cur, x_next, cot_cur, cot_next))
    grad_weights = total * (1.0 / math.sqrt(SEQS * SEQUENCE_TOKENS))
    return (x_prev, grad_cur, grad_weights)
```

```python
import functools
import math

import jax
import jax.numpy as jnp
from jax import lax
from jax.experimental import pallas as pl
from jax.experimental.pallas import tpu as pltpu
from jax.sharding import PartitionSpec as P

QUERY_HEADS = 8
KEY_VALUE_HEADS = 2
HEAD_SIZE = 128
WINDOW_TOKENS = 1024


EPS = 1e-05


MESH = pl.DeviceIdType.MESH


def gather_kernel(fsdp_count, q_in, kv_in, o_in, q_out, kv_out, o_out, own_sem, send_sem, recv_sem):
    ctx_at = lax.axis_index("ctx")
    fsdp_at = lax.axis_index("fsdp")
    half_at = lax.rem(ctx_at, 2)
    side = ctx_at + 1 - 2 * half_at
    core = fsdp_at + 1 - 2 * lax.rem(fsdp_at, 2)
    across = lax.rem(fsdp_at + fsdp_count // 2, fsdp_count)
    across_core = lax.rem(core + fsdp_count // 2, fsdp_count)
    ins, outs = ((q_in, kv_in, o_in), (q_out, kv_out, o_out))
    rows = q_in.shape[0]
    half = rows // 2
    pieces = []
    for index in (1, 0, 2):
        cuts = 1 if index == 1 else 2
        for cut in range(cuts):
            pieces.append((index, cut * (half // cuts), half // cuts))
    count = len(pieces)

    barrier = pltpu.get_barrier_semaphore()
    for target in ((ctx_at, core), (ctx_at, across), (side, fsdp_at)):
        pl.semaphore_signal(barrier, inc=1, device_id=target, device_id_type=MESH)
    pl.semaphore_wait(barrier, 3)

    def at(ref, owner, which, piece):
        _, start, size = piece
        return ref.at[pl.ds(pl.multiple_of(owner * rows + which * half + start, 128), size)]

    def remote(src, dst, slot, target):
        return pltpu.make_async_remote_copy(
            src_ref=src, dst_ref=dst, send_sem=send_sem.at[slot], recv_sem=recv_sem.at[slot],
            device_id=target, device_id_type=MESH,
        )

    y_copies = []
    for i, piece in enumerate(pieces):
        index, start, size = piece
        copy = remote(
            ins[index].at[pl.ds(pl.multiple_of(half_at * half + start, 128), size)],
            at(outs[index], fsdp_at, half_at, piece), i, (ctx_at, across),
        )
        copy.start()
        y_copies.append(copy)
    own_copies, core_copies = ([], [])
    for index in (1, 0, 2):
        place = outs[index].at[pl.ds(pl.multiple_of(fsdp_at * rows, 128), rows)]
        copy = remote(ins[index], place, 4 * count + index, (ctx_at, core))
        copy.start()
        core_copies.append(copy)
        copy = pltpu.make_async_copy(ins[index], place, own_sem.at[index])
        copy.start()
        own_copies.append(copy)
    x_copies = []
    for i, piece in enumerate(pieces):
        out = outs[piece[0]]
        here = at(out, across, half_at, piece)
        remote(here, here, i, (ctx_at, across)).wait_recv()
        copy = remote(here, here, count + i, (side, fsdp_at))
        copy.start()
        x_copies.append(copy)
        copy = remote(here, here, 2 * count + i, (ctx_at, core))
        copy.start()
        core_copies.append(copy)
    for i, piece in enumerate(pieces):
        here = at(outs[piece[0]], across, 1 - half_at, piece)
        remote(here, here, count + i, (side, fsdp_at)).wait_recv()
        copy = remote(here, here, 3 * count + i, (ctx_at, core))
        copy.start()
        core_copies.append(copy)
    for i, piece in enumerate(pieces):
        for level, which in ((2, half_at), (3, 1 - half_at)):
            here = at(outs[piece[0]], across_core, which, piece)
            remote(here, here, level * count + i, (ctx_at, core)).wait_recv()
    for index in range(3):
        place = outs[index].at[pl.ds(pl.multiple_of(core * rows, 128), rows)]
        remote(ins[index], place, 4 * count + index, (ctx_at, core)).wait_recv()
    for copy in y_copies + x_copies + core_copies:
        copy.wait_send()
    for copy in own_copies:
        copy.wait()


def gather_weights(w_q, w_kv, w_out):
    count = lax.axis_size("fsdp")
    shapes = [
        jax.ShapeDtypeStruct((count * w.shape[0], w.shape[1]), w.dtype) for w in (w_q, w_kv, w_out)
    ]
    slots = 4 * 5 + 3
    return pl.pallas_call(
        functools.partial(gather_kernel, count),
        out_shape=shapes,
        in_specs=[pl.BlockSpec(memory_space=pl.ANY)] * 3,
        out_specs=[pl.BlockSpec(memory_space=pl.ANY)] * 3,
        scratch_shapes=[
            pltpu.SemaphoreType.DMA((3,)),
            pltpu.SemaphoreType.DMA((slots,)),
            pltpu.SemaphoreType.DMA((slots,)),
        ],
        compiler_params=pltpu.CompilerParams(collective_id=0, has_side_effects=True),
        name="gather_weights",
    )(w_q, w_kv, w_out)


def reduce_plan(ctx_count, fsdp_count):
    ctx_bits = [("ctx", 1 << i) for i in range(ctx_count.bit_length() - 1)]
    fsdp_bits = [("fsdp", 1 << i) for i in range(fsdp_count.bit_length() - 1)]
    core, rest = (fsdp_bits[0], fsdp_bits[1:])
    order_a = rest + ctx_bits
    order_b = ctx_bits + rest
    order_c = ctx_bits[1:2] + rest + ctx_bits[:1] + ctx_bits[2:]
    return core, order_a, order_b, order_c


def reduce_parts(widths):
    q_width, kv_width, o_width = widths
    tail = 128
    return (
        (0, 0, q_width - tail, 0),
        (2, 0, o_width - tail, 1),
        (1, 0, kv_width, 2),
        (0, q_width - tail, tail, 2),
        (2, o_width - tail, tail, 2),
    )


def reduce_kernel(ctx_count, fsdp_count, parts, scale, *refs):
    terms, out_ref, refs = (refs[:3], refs[3], refs[4:])
    core, *orders = reduce_plan(ctx_count, fsdp_count)
    stages = len(orders[0])
    accs, recvs = ([], [])
    for _ in parts:
        accs.append(refs[: stages])
        recvs.append(refs[stages : 2 * stages + 1])
        refs = refs[2 * stages + 1 :]
    own_sem, send_sem, recv_sem = refs
    place = {"ctx": lax.axis_index("ctx"), "fsdp": lax.axis_index("fsdp")}
    count = ctx_count * fsdp_count
    block = terms[0].shape[0] // count
    offsets = (0, terms[0].shape[1], terms[0].shape[1] + terms[1].shape[1])

    def my_bit(bit):
        return lax.rem(place[bit[0]] // bit[1], 2)

    def partner(bit):
        flipped = place[bit[0]] + bit[1] * (1 - 2 * my_bit(bit))
        return (flipped, place["fsdp"]) if bit[0] == "ctx" else (place["ctx"], flipped)

    barrier = pltpu.get_barrier_semaphore()
    for bit in [core] + orders[0]:
        pl.semaphore_signal(barrier, inc=1, device_id=partner(bit), device_id_type=MESH)
    pl.semaphore_wait(barrier, stages + 1)

    half_blocks = count // 2
    for p, (index, start, width, order) in enumerate(parts):
        columns = pl.ds(start, width)

        def one(j, carry):
            owner = 0
            for i, bit in enumerate(orders[order]):
                digit = lax.rem(j // (half_blocks >> (i + 1)), 2)
                owner = owner + digit * bit[1] * (fsdp_count if bit[0] == "ctx" else 1)
            slot = pl.ds(pl.multiple_of(j * block, block), block)

            def rows(core_bit):
                return pl.ds(pl.multiple_of((owner + core_bit * core[1]) * block, block), block)

            pltpu.make_async_remote_copy(
                src_ref=terms[index].at[rows(1 - my_bit(core)), columns],
                dst_ref=recvs[p][0].at[slot],
                send_sem=send_sem.at[p, 0], recv_sem=recv_sem.at[p, 0],
                device_id=partner(core), device_id_type=MESH,
            ).start()
            pltpu.make_async_copy(
                terms[index].at[rows(my_bit(core)), columns], accs[p][0].at[slot], own_sem.at[p]
            ).start()
            return carry

        lax.fori_loop(0, half_blocks, one, 0)

    def add(target, first, base, second, size, last):
        step = min(size, 64)

        def body(i, carry):
            at = pl.multiple_of(i * step, step)
            value = first[pl.ds(pl.multiple_of(base + at, step), step)].astype(jnp.float32)
            value = value + second[pl.ds(at, step)].astype(jnp.float32)
            if last is None:
                target[pl.ds(at, step)] = value.astype(target.dtype)
            else:
                target[pl.ds(at, step), last] = value * scale
            return carry

        lax.fori_loop(0, size // step, body, 0)

    half_rows = half_blocks * block
    sends, latest = ([], {})
    for stage in range(stages + 1):
        size = half_rows >> stage
        for p, (index, start, width, order) in enumerate(parts):
            if stage == 0:
                whole = terms[index].at[pl.ds(0, half_rows), pl.ds(start, width)]
                pltpu.make_async_copy(whole, accs[p][0], own_sem.at[p]).wait()
                copy = pltpu.make_async_remote_copy(
                    src_ref=whole, dst_ref=recvs[p][0],
                    send_sem=send_sem.at[p, 0], recv_sem=recv_sem.at[p, 0],
                    device_id=partner(core), device_id_type=MESH,
                )
                copy.wait_recv()
                sends.append(copy)
                target, base, source = (accs[p][0], 0, accs[p][0])
            else:
                bit = orders[order][stage - 1]
                latest[p].wait_recv()
                source = accs[p][stage - 1]
                base = my_bit(bit) * size
                target = accs[p][stage] if stage < stages else out_ref
            last = pl.ds(offsets[index] + start, width) if stage == stages else None
            add(target, source, base, recvs[p][stage], size, last)
            if stage < stages:
                bit = orders[order][stage]
                send_from = pl.multiple_of((1 - my_bit(bit)) * (size // 2), size // 2)
                copy = pltpu.make_async_remote_copy(
                    src_ref=target.at[pl.ds(send_from, size // 2)],
                    dst_ref=recvs[p][stage + 1],
                    send_sem=send_sem.at[p, stage + 1], recv_sem=recv_sem.at[p, stage + 1],
                    device_id=partner(bit), device_id_type=MESH,
                )
                copy.start()
                latest[p] = copy
                sends.append(copy)
    for copy in sends:
        copy.wait_send()


def reduce_terms(term_q, term_kv, term_o, scale):
    ctx_count, fsdp_count = (lax.axis_size("ctx"), lax.axis_size("fsdp"))
    terms = (term_q, term_kv, term_o)
    widths = [t.shape[1] for t in terms]
    parts = reduce_parts(widths)
    count = ctx_count * fsdp_count
    block = term_q.shape[0] // count
    stages = count.bit_length() - 2
    scratch = []
    for _, _, width, _ in parts:
        half_rows = count // 2 * block
        for stage in range(stages):
            scratch.append(pltpu.VMEM((half_rows >> stage, width), jnp.bfloat16))
        for stage in range(stages + 1):
            scratch.append(pltpu.VMEM((half_rows >> stage, width), jnp.bfloat16))
    scratch += [
        pltpu.SemaphoreType.DMA((len(parts),)),
        pltpu.SemaphoreType.DMA((len(parts), stages + 1)),
        pltpu.SemaphoreType.DMA((len(parts), stages + 1)),
    ]
    return pl.pallas_call(
        functools.partial(reduce_kernel, ctx_count, fsdp_count, parts, scale),
        out_shape=jax.ShapeDtypeStruct((block, sum(widths)), jnp.float32),
        in_specs=[pl.BlockSpec(memory_space=pl.ANY)] * 3,
        out_specs=pl.BlockSpec(memory_space=pltpu.VMEM),
        scratch_shapes=scratch,
        compiler_params=pltpu.CompilerParams(
            collective_id=1, has_side_effects=True, vmem_limit_bytes=40 * 1024 * 1024
        ),
        name="reduce_terms",
    )(*terms)


def from_behind(value, axis, steps):
    count = lax.axis_size(axis)
    leading, last = (max(0, -steps), min(count, count - steps))
    return lax.ppermute(value, axis, [(source, source + steps) for source in range(leading, last)])


def normalize(rows):
    values = rows.astype(jnp.float32)
    inv_rms = lax.rsqrt(jnp.mean(values * values, axis=-1, keepdims=True) + EPS)
    return (values * inv_rms, inv_rms)


def head_block(items, allowed):
    quer3, keys2, vals2, grad3 = items
    scale = 1.0 / math.sqrt(HEAD_SIZE)
    scores = jnp.einsum("imd,jd->mij", quer3, keys2, preferred_element_type=jnp.float32) * scale
    scores = jnp.where(allowed[None], scores, -jnp.inf)
    top = jnp.max(scores, axis=-1, keepdims=True)
    expo = jnp.exp(scores - top)
    probs = expo / jnp.sum(expo, axis=-1, keepdims=True)
    probs_low = probs.astype(jnp.bfloat16)
    attended = jnp.einsum("mij,jd->imd", probs_low, vals2, preferred_element_type=jnp.float32)
    grad_probs = jnp.einsum("imd,jd->mij", grad3, vals2, preferred_element_type=jnp.float32)
    delta = jnp.einsum("imd,imd->mi", grad3.astype(jnp.float32), attended)
    grad_scores = (probs * (grad_probs - delta[..., None]) * scale).astype(jnp.bfloat16)
    grad_query = jnp.einsum("mij,jd->imd", grad_scores, keys2, preferred_element_type=jnp.float32)
    key_gradient = jnp.einsum("mij,imd->jd", grad_scores, quer3, preferred_element_type=jnp.float32)
    value_gradient = jnp.einsum("mij,imd->jd", probs_low, grad3, preferred_element_type=jnp.float32)
    return (
        attended.astype(jnp.bfloat16),
        grad_query.astype(jnp.bfloat16),
        key_gradient.astype(jnp.bfloat16),
        value_gradient.astype(jnp.bfloat16),
    )


def window_block(query_rows, key_value_pairs, output_gradient, base):
    window_extent = key_value_pairs.shape[0]
    element_count = query_rows.shape[0]
    query_group = QUERY_HEADS // KEY_VALUE_HEADS
    query_pos = base + jnp.arange(element_count, dtype=jnp.int32)
    key_pos = base - WINDOW_TOKENS + jnp.arange(window_extent, dtype=jnp.int32)
    offset = query_pos[:, None] - key_pos[None, :]
    allowed = (offset >= 0) & (offset < WINDOW_TOKENS) & (key_pos[None, :] >= 0)
    query_grouped = query_rows.reshape(
        element_count, KEY_VALUE_HEADS, query_group, HEAD_SIZE
    ).transpose(1, 0, 2, 3)
    gradient_grouped = output_gradient.reshape(
        element_count, KEY_VALUE_HEADS, query_group, HEAD_SIZE
    ).transpose(1, 0, 2, 3)
    key_tensor = (
        key_value_pairs[:, : KEY_VALUE_HEADS * HEAD_SIZE]
        .reshape(window_extent, KEY_VALUE_HEADS, HEAD_SIZE)
        .transpose(1, 0, 2)
    )
    value_tensor = (
        key_value_pairs[:, KEY_VALUE_HEADS * HEAD_SIZE :]
        .reshape(window_extent, KEY_VALUE_HEADS, HEAD_SIZE)
        .transpose(1, 0, 2)
    )

    def per_head(items):
        return head_block(items, allowed)

    attended, grad_query, key_gradient, value_gradient = lax.map(
        per_head, (query_grouped, key_tensor, value_tensor, gradient_grouped)
    )
    attended = attended.transpose(1, 0, 2, 3).reshape(element_count, QUERY_HEADS * HEAD_SIZE)
    grad_query = grad_query.transpose(1, 0, 2, 3).reshape(element_count, QUERY_HEADS * HEAD_SIZE)
    key_gradient = key_gradient.transpose(1, 0, 2).reshape(
        window_extent, KEY_VALUE_HEADS * HEAD_SIZE
    )
    value_gradient = value_gradient.transpose(1, 0, 2).reshape(
        window_extent, KEY_VALUE_HEADS * HEAD_SIZE
    )
    value_partial_sum = jnp.concatenate([key_gradient, value_gradient], 1)
    return (attended, grad_query, value_partial_sum)


def shards(x_cur, x_next, cot_cur, cot_next, w_q, w_kv, w_out):
    full_q, full_kv, full_out = gather_weights(w_q, w_kv, w_out)
    seq_count, shard, width = x_cur.shape
    base = lax.axis_index("ctx") * shard
    preds = WINDOW_TOKENS // shard
    normed, inv_rms = normalize(x_cur)
    hidden = normed.astype(jnp.bfloat16)
    query_rows = jnp.einsum(
        "sid,dc->sic", hidden, full_q, preferred_element_type=jnp.float32
    ).astype(jnp.bfloat16)
    key_value_pairs = jnp.einsum(
        "sid,dc->sic", hidden, full_kv, preferred_element_type=jnp.float32
    ).astype(jnp.bfloat16)
    grad_attn = (
        2.0 * jnp.einsum("sid,dc->sic", cot_next, full_out, preferred_element_type=jnp.float32)
    ).astype(jnp.bfloat16)
    earlier = []
    for hop in range(1, preds + 1):
        earlier.append(from_behind(key_value_pairs, "ctx", hop))
    window_keys = jnp.concatenate(earlier[::-1] + [key_value_pairs], axis=1)

    def per_sequence(items):
        q_rows, kv_rows, g_rows = items
        return window_block(q_rows, kv_rows, g_rows, base)

    attended, grad_query, value_partial_sum = lax.map(
        per_sequence, (query_rows, window_keys, grad_attn)
    )
    owned = value_partial_sum[:, WINDOW_TOKENS:].astype(jnp.float32)
    for hop in range(1, preds + 1):
        piece = value_partial_sum[
            :, WINDOW_TOKENS - hop * shard : WINDOW_TOKENS - (hop - 1) * shard
        ]
        owned = owned + from_behind(piece, "ctx", -hop).astype(jnp.float32)
    grad_kv = owned.astype(jnp.bfloat16)
    layer_out = jnp.einsum("sic,dc->sid", attended, full_out, preferred_element_type=jnp.float32)
    x_prev = (x_next.astype(jnp.float32) - 2.0 * layer_out).astype(jnp.bfloat16)
    grad_hidden = jnp.einsum("sic,dc->sid", grad_query, full_q, preferred_element_type=jnp.float32)
    grad_hidden = grad_hidden + jnp.einsum(
        "sic,dc->sid", grad_kv, full_kv, preferred_element_type=jnp.float32
    )
    grad_x = inv_rms * (
        grad_hidden - normed * jnp.mean(grad_hidden * normed, axis=-1, keepdims=True)
    )
    grad_cur = (cot_cur.astype(jnp.float32) + grad_x).astype(jnp.bfloat16)
    hidden_rows = hidden.reshape(seq_count * shard, width)
    cot_rows = cot_next.reshape(seq_count * shard, width)
    query_left = grad_query.reshape(seq_count * shard, -1)
    keyval_left = grad_kv.reshape(seq_count * shard, -1)
    attended_rows = attended.reshape(seq_count * shard, -1)
    contract_rows = (((0,), (0,)), ((), ()))
    ctx_count = lax.axis_size("ctx")
    fsdp_count = lax.axis_size("fsdp")
    term_q, term_kv = (
        lax.dot_general(hidden_rows, left, contract_rows, preferred_element_type=jnp.float32)
        for left in (query_left, keyval_left)
    )
    term_out = 2.0 * lax.dot_general(
        cot_rows, attended_rows, contract_rows, preferred_element_type=jnp.float32
    )
    token_total = seq_count * shard * ctx_count * fsdp_count
    grad_weights = reduce_terms(
        term_q.astype(jnp.bfloat16),
        term_kv.astype(jnp.bfloat16),
        term_out.astype(jnp.bfloat16),
        1.0 / math.sqrt(token_total),
    )
    return (x_prev, grad_cur, grad_weights)


def solution(mesh):
    in_specs = (
        P("fsdp", "ctx", None),
        P("fsdp", "ctx", None),
        P("fsdp", "ctx", None),
        P("fsdp", "ctx", None),
        P("fsdp", None),
        P("fsdp", None),
        P("fsdp", None),
    )
    out_specs = (P("fsdp", "ctx", None), P("fsdp", "ctx", None), P(("ctx", "fsdp"), None))
    return jax.shard_map(shards, mesh=mesh, in_specs=in_specs, out_specs=out_specs, check_vma=False)
```

```python
import functools
import math

import jax
import jax.numpy as jnp
from jax import lax
from jax.experimental import pallas as pl
from jax.experimental.pallas import tpu as pltpu
from jax.sharding import PartitionSpec as P

QUERY_HEADS = 8
KEY_VALUE_HEADS = 2
HEAD_SIZE = 128
WINDOW_TOKENS = 1024


EPS = 1e-05


MESH = pl.DeviceIdType.MESH


def gather_kernel(fsdp_count, q_in, kv_in, o_in, q_out, kv_out, o_out, own_sem, send_sem, recv_sem):
    ctx_at = lax.axis_index("ctx")
    fsdp_at = lax.axis_index("fsdp")
    half_at = lax.rem(ctx_at, 2)
    side = ctx_at + 1 - 2 * half_at
    core = fsdp_at + 1 - 2 * lax.rem(fsdp_at, 2)
    across = lax.rem(fsdp_at + fsdp_count // 2, fsdp_count)
    across_core = lax.rem(core + fsdp_count // 2, fsdp_count)
    ins, outs = ((q_in, kv_in, o_in), (q_out, kv_out, o_out))
    rows = q_in.shape[0]
    half = rows // 2
    pieces = []
    for index in (1, 0, 2):
        cuts = 1 if index == 1 else 2
        for cut in range(cuts):
            pieces.append((index, cut * (half // cuts), half // cuts))
    count = len(pieces)

    barrier = pltpu.get_barrier_semaphore()
    for target in ((ctx_at, core), (ctx_at, across), (side, fsdp_at)):
        pl.semaphore_signal(barrier, inc=1, device_id=target, device_id_type=MESH)
    pl.semaphore_wait(barrier, 3)

    def at(ref, owner, which, piece):
        _, start, size = piece
        return ref.at[pl.ds(pl.multiple_of(owner * rows + which * half + start, 128), size)]

    def remote(src, dst, slot, target):
        return pltpu.make_async_remote_copy(
            src_ref=src, dst_ref=dst, send_sem=send_sem.at[slot], recv_sem=recv_sem.at[slot],
            device_id=target, device_id_type=MESH,
        )

    y_copies = []
    for i, piece in enumerate(pieces):
        index, start, size = piece
        copy = remote(
            ins[index].at[pl.ds(pl.multiple_of(half_at * half + start, 128), size)],
            at(outs[index], fsdp_at, half_at, piece), i, (ctx_at, across),
        )
        copy.start()
        y_copies.append(copy)
    own_copies, core_copies = ([], [])
    for index in (1, 0, 2):
        place = outs[index].at[pl.ds(pl.multiple_of(fsdp_at * rows, 128), rows)]
        copy = remote(ins[index], place, 4 * count + index, (ctx_at, core))
        copy.start()
        core_copies.append(copy)
        copy = pltpu.make_async_copy(ins[index], place, own_sem.at[index])
        copy.start()
        own_copies.append(copy)
    x_copies = []
    for i, piece in enumerate(pieces):
        out = outs[piece[0]]
        here = at(out, across, half_at, piece)
        remote(here, here, i, (ctx_at, across)).wait_recv()
        copy = remote(here, here, count + i, (side, fsdp_at))
        copy.start()
        x_copies.append(copy)
        copy = remote(here, here, 2 * count + i, (ctx_at, core))
        copy.start()
        core_copies.append(copy)
    for i, piece in enumerate(pieces):
        here = at(outs[piece[0]], across, 1 - half_at, piece)
        remote(here, here, count + i, (side, fsdp_at)).wait_recv()
        copy = remote(here, here, 3 * count + i, (ctx_at, core))
        copy.start()
        core_copies.append(copy)
    for i, piece in enumerate(pieces):
        for level, which in ((2, half_at), (3, 1 - half_at)):
            here = at(outs[piece[0]], across_core, which, piece)
            remote(here, here, level * count + i, (ctx_at, core)).wait_recv()
    for index in range(3):
        place = outs[index].at[pl.ds(pl.multiple_of(core * rows, 128), rows)]
        remote(ins[index], place, 4 * count + index, (ctx_at, core)).wait_recv()
    for copy in y_copies + x_copies + core_copies:
        copy.wait_send()
    for copy in own_copies:
        copy.wait()


def gather_weights(w_q, w_kv, w_out):
    count = lax.axis_size("fsdp")
    shapes = [
        jax.ShapeDtypeStruct((count * w.shape[0], w.shape[1]), w.dtype) for w in (w_q, w_kv, w_out)
    ]
    slots = 4 * 5 + 3
    return pl.pallas_call(
        functools.partial(gather_kernel, count),
        out_shape=shapes,
        in_specs=[pl.BlockSpec(memory_space=pl.ANY)] * 3,
        out_specs=[pl.BlockSpec(memory_space=pltpu.VMEM)] * 3,
        scratch_shapes=[
            pltpu.SemaphoreType.DMA((3,)),
            pltpu.SemaphoreType.DMA((slots,)),
            pltpu.SemaphoreType.DMA((slots,)),
        ],
        compiler_params=pltpu.CompilerParams(
            collective_id=0, has_side_effects=True, vmem_limit_bytes=40 * 1024 * 1024
        ),
        name="gather_weights",
    )(w_q, w_kv, w_out)


def reduce_plan(ctx_count, fsdp_count):
    ctx_bits = [("ctx", 1 << i) for i in range(ctx_count.bit_length() - 1)]
    fsdp_bits = [("fsdp", 1 << i) for i in range(fsdp_count.bit_length() - 1)]
    core, rest = (fsdp_bits[0], fsdp_bits[1:])
    order_a = rest + ctx_bits
    order_b = ctx_bits + rest
    order_c = ctx_bits[1:2] + rest + ctx_bits[:1] + ctx_bits[2:]
    return core, order_a, order_b, order_c


def reduce_parts(widths):
    q_width, kv_width, o_width = widths
    tail = 128
    return (
        (0, 0, q_width - tail, 0),
        (2, 0, o_width - tail, 1),
        (1, 0, kv_width, 2),
        (0, q_width - tail, tail, 2),
        (2, o_width - tail, tail, 2),
    )


def reduce_kernel(ctx_count, fsdp_count, parts, scale, *refs):
    terms, out_ref, refs = (refs[:3], refs[3], refs[4:])
    core, *orders = reduce_plan(ctx_count, fsdp_count)
    stages = len(orders[0])
    accs, recvs = ([], [])
    for _ in parts:
        accs.append(refs[: stages])
        recvs.append(refs[stages : 2 * stages + 1])
        refs = refs[2 * stages + 1 :]
    own_sem, send_sem, recv_sem = refs
    place = {"ctx": lax.axis_index("ctx"), "fsdp": lax.axis_index("fsdp")}
    count = ctx_count * fsdp_count
    block = terms[0].shape[0] // count
    offsets = (0, terms[0].shape[1], terms[0].shape[1] + terms[1].shape[1])

    def my_bit(bit):
        return lax.rem(place[bit[0]] // bit[1], 2)

    def partner(bit):
        flipped = place[bit[0]] + bit[1] * (1 - 2 * my_bit(bit))
        return (flipped, place["fsdp"]) if bit[0] == "ctx" else (place["ctx"], flipped)

    barrier = pltpu.get_barrier_semaphore()
    for bit in [core] + orders[0]:
        pl.semaphore_signal(barrier, inc=1, device_id=partner(bit), device_id_type=MESH)
    pl.semaphore_wait(barrier, stages + 1)

    half_blocks = count // 2
    for p, (index, start, width, order) in enumerate(parts):
        columns = pl.ds(start, width)

        def one(j, carry):
            owner = 0
            for i, bit in enumerate(orders[order]):
                digit = lax.rem(j // (half_blocks >> (i + 1)), 2)
                owner = owner + digit * bit[1] * (fsdp_count if bit[0] == "ctx" else 1)
            slot = pl.ds(pl.multiple_of(j * block, block), block)

            def rows(core_bit):
                return pl.ds(pl.multiple_of((owner + core_bit * core[1]) * block, block), block)

            pltpu.make_async_remote_copy(
                src_ref=terms[index].at[rows(1 - my_bit(core)), columns],
                dst_ref=recvs[p][0].at[slot],
                send_sem=send_sem.at[p, 0], recv_sem=recv_sem.at[p, 0],
                device_id=partner(core), device_id_type=MESH,
            ).start()
            pltpu.make_async_copy(
                terms[index].at[rows(my_bit(core)), columns], accs[p][0].at[slot], own_sem.at[p]
            ).start()
            return carry

        lax.fori_loop(0, half_blocks, one, 0)

    def add(target, first, base, second, size, last):
        step = min(size, 64)

        def body(i, carry):
            at = pl.multiple_of(i * step, step)
            value = first[pl.ds(pl.multiple_of(base + at, step), step)].astype(jnp.float32)
            value = value + second[pl.ds(at, step)].astype(jnp.float32)
            if last is None:
                target[pl.ds(at, step)] = value.astype(target.dtype)
            else:
                target[pl.ds(at, step), last] = value * scale
            return carry

        lax.fori_loop(0, size // step, body, 0)

    half_rows = half_blocks * block
    sends, latest = ([], {})
    for stage in range(stages + 1):
        size = half_rows >> stage
        for p, (index, start, width, order) in enumerate(parts):
            if stage == 0:
                whole = terms[index].at[pl.ds(0, half_rows), pl.ds(start, width)]
                pltpu.make_async_copy(whole, accs[p][0], own_sem.at[p]).wait()
                copy = pltpu.make_async_remote_copy(
                    src_ref=whole, dst_ref=recvs[p][0],
                    send_sem=send_sem.at[p, 0], recv_sem=recv_sem.at[p, 0],
                    device_id=partner(core), device_id_type=MESH,
                )
                copy.wait_recv()
                sends.append(copy)
                target, base, source = (accs[p][0], 0, accs[p][0])
            else:
                bit = orders[order][stage - 1]
                latest[p].wait_recv()
                source = accs[p][stage - 1]
                base = my_bit(bit) * size
                target = accs[p][stage] if stage < stages else out_ref
            last = pl.ds(offsets[index] + start, width) if stage == stages else None
            add(target, source, base, recvs[p][stage], size, last)
            if stage < stages:
                bit = orders[order][stage]
                send_from = pl.multiple_of((1 - my_bit(bit)) * (size // 2), size // 2)
                copy = pltpu.make_async_remote_copy(
                    src_ref=target.at[pl.ds(send_from, size // 2)],
                    dst_ref=recvs[p][stage + 1],
                    send_sem=send_sem.at[p, stage + 1], recv_sem=recv_sem.at[p, stage + 1],
                    device_id=partner(bit), device_id_type=MESH,
                )
                copy.start()
                latest[p] = copy
                sends.append(copy)
    for copy in sends:
        copy.wait_send()


def reduce_terms(term_q, term_kv, term_o, scale):
    ctx_count, fsdp_count = (lax.axis_size("ctx"), lax.axis_size("fsdp"))
    terms = (term_q, term_kv, term_o)
    widths = [t.shape[1] for t in terms]
    parts = reduce_parts(widths)
    count = ctx_count * fsdp_count
    block = term_q.shape[0] // count
    stages = count.bit_length() - 2
    scratch = []
    for _, _, width, _ in parts:
        half_rows = count // 2 * block
        for stage in range(stages):
            scratch.append(pltpu.VMEM((half_rows >> stage, width), jnp.bfloat16))
        for stage in range(stages + 1):
            scratch.append(pltpu.VMEM((half_rows >> stage, width), jnp.bfloat16))
    scratch += [
        pltpu.SemaphoreType.DMA((len(parts),)),
        pltpu.SemaphoreType.DMA((len(parts), stages + 1)),
        pltpu.SemaphoreType.DMA((len(parts), stages + 1)),
    ]
    return pl.pallas_call(
        functools.partial(reduce_kernel, ctx_count, fsdp_count, parts, scale),
        out_shape=jax.ShapeDtypeStruct((block, sum(widths)), jnp.float32),
        in_specs=[pl.BlockSpec(memory_space=pl.ANY)] * 3,
        out_specs=pl.BlockSpec(memory_space=pltpu.VMEM),
        scratch_shapes=scratch,
        compiler_params=pltpu.CompilerParams(
            collective_id=1, has_side_effects=True, vmem_limit_bytes=40 * 1024 * 1024
        ),
        name="reduce_terms",
    )(*terms)


def from_behind(value, axis, steps):
    count = lax.axis_size(axis)
    leading, last = (max(0, -steps), min(count, count - steps))
    return lax.ppermute(value, axis, [(source, source + steps) for source in range(leading, last)])


def normalize(rows):
    values = rows.astype(jnp.float32)
    inv_rms = lax.rsqrt(jnp.mean(values * values, axis=-1, keepdims=True) + EPS)
    return (values * inv_rms, inv_rms)


def attend_kernel(preds, q_ref, g_ref, *refs):
    count = preds + 1
    keys, values, refs = (refs[:count], refs[count : 2 * count], refs[2 * count :])
    attended_ref, dq_ref, dkv_refs, refs = (refs[0], refs[1], refs[2 : 2 + count], refs[2 + count :])
    bias, work, dk_acc, dv_acc = refs
    shard = q_ref.shape[0]
    group = pl.program_id(0)
    heads = q_ref.shape[1] // HEAD_SIZE
    scale = 1.0 / math.sqrt(HEAD_SIZE)
    contract_last = (((1,), (1,)), ((), ()))
    contract_mid = (((1,), (0,)), ((), ()))

    def dot(a, b, dims):
        return lax.dot_general(a, b, dims, preferred_element_type=jnp.float32)

    @pl.when(group == 0)
    def _():
        base = lax.axis_index("ctx") * shard
        key_at = lax.broadcasted_iota(jnp.int32, (shard, shard), 0)
        query_at = lax.broadcasted_iota(jnp.int32, (shard, shard), 1)
        for block in range(count):
            key_pos = key_at + (block - preds) * shard
            offset = query_at - key_pos
            allowed = (offset >= 0) & (offset < WINDOW_TOKENS) & (key_pos + base >= 0)
            bias[block] = jnp.where(allowed, 0.0, -jnp.inf)

    keys_t = [k[...].T for k in keys]
    values_t = [v[...].T for v in values]
    for head in range(heads):
        columns = slice(head * HEAD_SIZE, (head + 1) * HEAD_SIZE)
        q = q_ref[:, columns]
        g = g_ref[:, columns]
        slot = head % 2
        top = None
        for block in range(count):
            scores = dot(keys[block][...], q, contract_last) * (scale * math.log2(math.e))
            scores = scores + bias[block]
            work[slot, block] = scores
            peak = jnp.max(scores, axis=0, keepdims=True)
            top = peak if top is None else jnp.maximum(top, peak)
        total = 0.0
        for block in range(count):
            expo = jnp.exp2(work[slot, block] - top)
            work[slot, block] = expo
            total = total + jnp.sum(expo, axis=0, keepdims=True)
        inverse = 1.0 / total
        attended_t = 0.0
        for block in range(count):
            probs = work[slot, block] * inverse
            work[slot, block] = probs
            probs_low = probs.astype(jnp.bfloat16)
            attended_t = attended_t + dot(values_t[block], probs_low, contract_mid)
            dv = dot(probs_low, g, contract_mid)
            dv_acc[block] = dv if head == 0 else dv_acc[block] + dv
        delta = jnp.sum(g.astype(jnp.float32).T * attended_t, axis=0, keepdims=True)
        attended_ref[:, columns] = attended_t.T.astype(jnp.bfloat16)
        dq_t = 0.0
        for block in range(count):
            grad_probs = dot(values[block][...], g, contract_last)
            grad_scores = work[slot, block] * (grad_probs - delta) * scale
            grad_scores = grad_scores.astype(jnp.bfloat16)
            dq_t = dq_t + dot(keys_t[block], grad_scores, contract_mid)
            dk = dot(grad_scores, q, contract_mid)
            dk_acc[block] = dk if head == 0 else dk_acc[block] + dk
        dq_ref[:, columns] = dq_t.T.astype(jnp.bfloat16)
    for block in range(count):
        at = pl.multiple_of(group * HEAD_SIZE, HEAD_SIZE)
        dkv_refs[block][:, pl.ds(at, HEAD_SIZE)] = dk_acc[block].astype(jnp.bfloat16)
        at = pl.multiple_of((KEY_VALUE_HEADS + group) * HEAD_SIZE, HEAD_SIZE)
        dkv_refs[block][:, pl.ds(at, HEAD_SIZE)] = dv_acc[block].astype(jnp.bfloat16)


def attend(query_rows, grad_rows, blocks):
    shard, width = query_rows.shape
    count = len(blocks)
    group_width = width // KEY_VALUE_HEADS
    query_spec = pl.BlockSpec((shard, group_width), lambda i: (0, i))
    key_spec = pl.BlockSpec((shard, HEAD_SIZE), lambda i: (0, i))
    value_spec = pl.BlockSpec((shard, HEAD_SIZE), lambda i: (0, KEY_VALUE_HEADS + i))
    pair_spec = pl.BlockSpec((shard, blocks[0].shape[1]), lambda i: (0, 0))
    wide = jax.ShapeDtypeStruct((shard, width), jnp.bfloat16)
    pair = jax.ShapeDtypeStruct(blocks[0].shape, jnp.bfloat16)
    flops = 10 * shard * shard * count * width
    return pl.pallas_call(
        functools.partial(attend_kernel, count - 1),
        grid=(KEY_VALUE_HEADS,),
        out_shape=[wide, wide] + [pair] * count,
        in_specs=[query_spec] * 2 + [key_spec] * count + [value_spec] * count,
        out_specs=[query_spec] * 2 + [pair_spec] * count,
        scratch_shapes=[
            pltpu.VMEM((count, shard, shard), jnp.float32),
            pltpu.VMEM((2, count, shard, shard), jnp.float32),
            pltpu.VMEM((count, shard, HEAD_SIZE), jnp.float32),
            pltpu.VMEM((count, shard, HEAD_SIZE), jnp.float32),
        ],
        compiler_params=pltpu.CompilerParams(vmem_limit_bytes=40 * 1024 * 1024),
        cost_estimate=pl.CostEstimate(
            flops=flops, bytes_accessed=4 * 1024 * 1024, transcendentals=shard * shard * count * 8
        ),
        name="attend",
    )(query_rows, grad_rows, *blocks, *blocks)


def shards(x_cur, x_next, cot_cur, cot_next, w_q, w_kv, w_out):
    full_q, full_kv, full_out = gather_weights(w_q, w_kv, w_out)
    seq_count, shard, width = x_cur.shape
    preds = WINDOW_TOKENS // shard
    normed, inv_rms = normalize(x_cur)
    hidden = normed.astype(jnp.bfloat16)
    query_rows = jnp.einsum(
        "sid,dc->sic", hidden, full_q, preferred_element_type=jnp.float32
    ).astype(jnp.bfloat16)
    key_value_pairs = jnp.einsum(
        "sid,dc->sic", hidden, full_kv, preferred_element_type=jnp.float32
    ).astype(jnp.bfloat16)
    grad_attn = (
        2.0 * jnp.einsum("sid,dc->sic", cot_next, full_out, preferred_element_type=jnp.float32)
    ).astype(jnp.bfloat16)
    earlier = []
    for hop in range(1, preds + 1):
        earlier.append(from_behind(key_value_pairs, "ctx", hop))
    results = []
    for seq in range(seq_count):
        window = [block[seq] for block in earlier[::-1]] + [key_value_pairs[seq]]
        results.append(attend(query_rows[seq], grad_attn[seq], window))
    attended, grad_query, *pieces = (jnp.stack(parts) for parts in zip(*results))
    owned = pieces[preds].astype(jnp.float32)
    for hop in range(1, preds + 1):
        owned = owned + from_behind(pieces[preds - hop], "ctx", -hop).astype(jnp.float32)
    grad_kv = owned.astype(jnp.bfloat16)
    layer_out = jnp.einsum("sic,dc->sid", attended, full_out, preferred_element_type=jnp.float32)
    x_prev = (x_next.astype(jnp.float32) - 2.0 * layer_out).astype(jnp.bfloat16)
    grad_hidden = jnp.einsum("sic,dc->sid", grad_query, full_q, preferred_element_type=jnp.float32)
    grad_hidden = grad_hidden + jnp.einsum(
        "sic,dc->sid", grad_kv, full_kv, preferred_element_type=jnp.float32
    )
    grad_x = inv_rms * (
        grad_hidden - normed * jnp.mean(grad_hidden * normed, axis=-1, keepdims=True)
    )
    grad_cur = (cot_cur.astype(jnp.float32) + grad_x).astype(jnp.bfloat16)
    hidden_rows = hidden.reshape(seq_count * shard, width)
    cot_rows = cot_next.reshape(seq_count * shard, width)
    query_left = grad_query.reshape(seq_count * shard, -1)
    keyval_left = grad_kv.reshape(seq_count * shard, -1)
    attended_rows = attended.reshape(seq_count * shard, -1)
    contract_rows = (((0,), (0,)), ((), ()))
    ctx_count = lax.axis_size("ctx")
    fsdp_count = lax.axis_size("fsdp")
    term_q, term_kv = (
        lax.dot_general(hidden_rows, left, contract_rows, preferred_element_type=jnp.float32)
        for left in (query_left, keyval_left)
    )
    term_out = 2.0 * lax.dot_general(
        cot_rows, attended_rows, contract_rows, preferred_element_type=jnp.float32
    )
    token_total = seq_count * shard * ctx_count * fsdp_count
    grad_weights = reduce_terms(
        term_q.astype(jnp.bfloat16),
        term_kv.astype(jnp.bfloat16),
        term_out.astype(jnp.bfloat16),
        1.0 / math.sqrt(token_total),
    )
    return (x_prev, grad_cur, grad_weights)


def solution(mesh):
    in_specs = (
        P("fsdp", "ctx", None),
        P("fsdp", "ctx", None),
        P("fsdp", "ctx", None),
        P("fsdp", "ctx", None),
        P("fsdp", None),
        P("fsdp", None),
        P("fsdp", None),
    )
    out_specs = (P("fsdp", "ctx", None), P("fsdp", "ctx", None), P(("ctx", "fsdp"), None))
    return jax.shard_map(shards, mesh=mesh, in_specs=in_specs, out_specs=out_specs, check_vma=False)
```

```python
import functools
import math

import jax
import jax.numpy as jnp
from jax import lax
from jax.experimental import pallas as pl
from jax.experimental.pallas import tpu as pltpu
from jax.sharding import PartitionSpec as P

QUERY_HEADS = 8
KEY_VALUE_HEADS = 2
HEAD_SIZE = 128
WINDOW_TOKENS = 1024


EPS = 1e-05


MESH = pl.DeviceIdType.MESH


def gather_kernel(fsdp_count, q_in, kv_in, o_in, q_out, kv_out, o_out, own_sem, send_sem, recv_sem):
    ctx_at = lax.axis_index("ctx")
    fsdp_at = lax.axis_index("fsdp")
    half_at = lax.rem(ctx_at, 2)
    side = ctx_at + 1 - 2 * half_at
    core = fsdp_at + 1 - 2 * lax.rem(fsdp_at, 2)
    across = lax.rem(fsdp_at + fsdp_count // 2, fsdp_count)
    across_core = lax.rem(core + fsdp_count // 2, fsdp_count)
    ins, outs = ((q_in, kv_in, o_in), (q_out, kv_out, o_out))
    rows = q_in.shape[0]
    half = rows // 2
    pieces = []
    for index in (1, 0, 2):
        cuts = 1 if index == 1 else 2
        for cut in range(cuts):
            pieces.append((index, cut * (half // cuts), half // cuts))
    count = len(pieces)

    barrier = pltpu.get_barrier_semaphore()
    for target in ((ctx_at, core), (ctx_at, across), (side, fsdp_at)):
        pl.semaphore_signal(barrier, inc=1, device_id=target, device_id_type=MESH)
    pl.semaphore_wait(barrier, 3)

    def at(ref, owner, which, piece):
        _, start, size = piece
        return ref.at[pl.ds(pl.multiple_of(owner * rows + which * half + start, 128), size)]

    def remote(src, dst, slot, target):
        return pltpu.make_async_remote_copy(
            src_ref=src, dst_ref=dst, send_sem=send_sem.at[slot], recv_sem=recv_sem.at[slot],
            device_id=target, device_id_type=MESH,
        )

    y_copies = []
    for i, piece in enumerate(pieces):
        index, start, size = piece
        copy = remote(
            ins[index].at[pl.ds(pl.multiple_of(half_at * half + start, 128), size)],
            at(outs[index], fsdp_at, half_at, piece), i, (ctx_at, across),
        )
        copy.start()
        y_copies.append(copy)
    own_copies, core_copies = ([], [])
    for index in (1, 0, 2):
        place = outs[index].at[pl.ds(pl.multiple_of(fsdp_at * rows, 128), rows)]
        copy = remote(ins[index], place, 4 * count + index, (ctx_at, core))
        copy.start()
        core_copies.append(copy)
        copy = pltpu.make_async_copy(ins[index], place, own_sem.at[index])
        copy.start()
        own_copies.append(copy)
    x_copies = []
    for i, piece in enumerate(pieces):
        out = outs[piece[0]]
        here = at(out, across, half_at, piece)
        remote(here, here, i, (ctx_at, across)).wait_recv()
        copy = remote(here, here, count + i, (side, fsdp_at))
        copy.start()
        x_copies.append(copy)
        copy = remote(here, here, 2 * count + i, (ctx_at, core))
        copy.start()
        core_copies.append(copy)
    for i, piece in enumerate(pieces):
        here = at(outs[piece[0]], across, 1 - half_at, piece)
        remote(here, here, count + i, (side, fsdp_at)).wait_recv()
        copy = remote(here, here, 3 * count + i, (ctx_at, core))
        copy.start()
        core_copies.append(copy)
    for i, piece in enumerate(pieces):
        for level, which in ((2, half_at), (3, 1 - half_at)):
            here = at(outs[piece[0]], across_core, which, piece)
            remote(here, here, level * count + i, (ctx_at, core)).wait_recv()
    for index in range(3):
        place = outs[index].at[pl.ds(pl.multiple_of(core * rows, 128), rows)]
        remote(ins[index], place, 4 * count + index, (ctx_at, core)).wait_recv()
    for copy in y_copies + x_copies + core_copies:
        copy.wait_send()
    for copy in own_copies:
        copy.wait()


def gather_weights(w_q, w_kv, w_out):
    count = lax.axis_size("fsdp")
    shapes = [
        jax.ShapeDtypeStruct((count * w.shape[0], w.shape[1]), w.dtype) for w in (w_q, w_kv, w_out)
    ]
    slots = 4 * 5 + 3
    return pl.pallas_call(
        functools.partial(gather_kernel, count),
        out_shape=shapes,
        in_specs=[pl.BlockSpec(memory_space=pl.ANY)] * 3,
        out_specs=[pl.BlockSpec(memory_space=pltpu.VMEM)] * 3,
        scratch_shapes=[
            pltpu.SemaphoreType.DMA((3,)),
            pltpu.SemaphoreType.DMA((slots,)),
            pltpu.SemaphoreType.DMA((slots,)),
        ],
        compiler_params=pltpu.CompilerParams(
            collective_id=0, has_side_effects=True, vmem_limit_bytes=40 * 1024 * 1024
        ),
        name="gather_weights",
    )(w_q, w_kv, w_out)


def reduce_plan(ctx_count, fsdp_count):
    ctx_bits = [("ctx", 1 << i) for i in range(ctx_count.bit_length() - 1)]
    fsdp_bits = [("fsdp", 1 << i) for i in range(fsdp_count.bit_length() - 1)]
    core, rest = (fsdp_bits[0], fsdp_bits[1:])
    order_a = rest + ctx_bits
    order_b = ctx_bits + rest
    order_c = ctx_bits[1:2] + rest + ctx_bits[:1] + ctx_bits[2:]
    return core, order_a, order_b, order_c


def reduce_parts(widths):
    q_width, kv_width, o_width = widths
    tail = 256
    half = kv_width // 2
    return (
        (0, 0, q_width - tail, 0),
        (2, 0, o_width - tail, 1),
        (0, q_width - tail, tail, 2),
        (2, o_width - tail, tail, 2),
        (1, 0, half, 0),
        (1, half, half, 1),
    )


def reduce_kernel(ctx_count, fsdp_count, preds, parts, scale, *refs):
    term_q, term_o, hidden_ref, refs = (refs[0], refs[1], refs[2], refs[3:])
    pieces, out_ref, grad_kv_ref, refs = (refs[: preds + 1], refs[preds + 1], refs[preds + 2], refs[preds + 3 :])
    arrived, kv_sum, term_kv, kv_send, kv_recv = refs[:5]
    refs = refs[5:]
    terms = (term_q, term_kv, term_o)
    core, *orders = reduce_plan(ctx_count, fsdp_count)
    stages = len(orders[0])
    accs, recvs = ([], [])
    for _ in parts:
        accs.append(refs[: stages])
        recvs.append(refs[stages : 2 * stages + 1])
        refs = refs[2 * stages + 1 :]
    own_sem, send_sem, recv_sem = refs
    place = {"ctx": lax.axis_index("ctx"), "fsdp": lax.axis_index("fsdp")}
    count = ctx_count * fsdp_count
    block = terms[0].shape[0] // count
    offsets = (0, terms[0].shape[1], terms[0].shape[1] + terms[1].shape[1])

    def my_bit(bit):
        return lax.rem(place[bit[0]] // bit[1], 2)

    def partner(bit):
        flipped = place[bit[0]] + bit[1] * (1 - 2 * my_bit(bit))
        return (flipped, place["fsdp"]) if bit[0] == "ctx" else (place["ctx"], flipped)

    barrier = pltpu.get_barrier_semaphore()
    for bit in [core] + orders[0]:
        pl.semaphore_signal(barrier, inc=1, device_id=partner(bit), device_id_type=MESH)
    ctx_at = place["ctx"]
    for hop in range(1, preds + 1):

        @pl.when(ctx_at + hop < ctx_count)
        def _():
            pl.semaphore_signal(
                barrier, inc=1, device_id=(ctx_at + hop, place["fsdp"]), device_id_type=MESH
            )

    pl.semaphore_wait(barrier, stages + 1 + jnp.minimum(ctx_at, preds))

    def piece_copy(hop, target):
        return pltpu.make_async_remote_copy(
            src_ref=pieces[preds - hop], dst_ref=arrived.at[hop - 1],
            send_sem=kv_send.at[hop - 1], recv_sem=kv_recv.at[hop - 1],
            device_id=(target, place["fsdp"]), device_id_type=MESH,
        )

    for hop in range(1, preds + 1):

        @pl.when(ctx_at >= hop)
        def _():
            piece_copy(hop, ctx_at - hop).start()

    half_blocks = count // 2

    def launch(p):
        index, start, width, order = parts[p]
        columns = pl.ds(start, width)

        def one(j, carry):
            owner = 0
            for i, bit in enumerate(orders[order]):
                digit = lax.rem(j // (half_blocks >> (i + 1)), 2)
                owner = owner + digit * bit[1] * (fsdp_count if bit[0] == "ctx" else 1)
            slot = pl.ds(pl.multiple_of(j * block, block), block)

            def rows(core_bit):
                return pl.ds(pl.multiple_of((owner + core_bit * core[1]) * block, block), block)

            pltpu.make_async_remote_copy(
                src_ref=terms[index].at[rows(1 - my_bit(core)), columns],
                dst_ref=recvs[p][0].at[slot],
                send_sem=send_sem.at[p, 0], recv_sem=recv_sem.at[p, 0],
                device_id=partner(core), device_id_type=MESH,
            ).start()
            pltpu.make_async_copy(
                terms[index].at[rows(my_bit(core)), columns], accs[p][0].at[slot], own_sem.at[p]
            ).start()
            return carry

        lax.fori_loop(0, half_blocks, one, 0)

    def add(target, first, base, second, size, last):
        step = min(size, 64)

        def body(i, carry):
            at = pl.multiple_of(i * step, step)
            value = first[pl.ds(pl.multiple_of(base + at, step), step)].astype(jnp.float32)
            value = value + second[pl.ds(at, step)].astype(jnp.float32)
            if last is None:
                target[pl.ds(at, step)] = value.astype(target.dtype)
            else:
                target[pl.ds(at, step), last] = value * scale
            return carry

        lax.fori_loop(0, size // step, body, 0)

    half_rows = half_blocks * block
    early = [p for p, part in enumerate(parts) if part[0] != 1]
    late = [p for p, part in enumerate(parts) if part[0] == 1]
    for p in early:
        launch(p)

    def own_keys():
        kv_sum[...] = pieces[preds][...].astype(jnp.float32)
        for hop in range(1, preds + 1):

            @pl.when(ctx_at + hop < ctx_count)
            def _():
                piece_copy(hop, ctx_at + hop).wait_recv()
                kv_sum[...] += arrived[hop - 1].astype(jnp.float32)

        grad_kv_ref[...] = kv_sum[...].astype(jnp.bfloat16)
        step = 256

        def body(i, carry):
            at = pl.ds(pl.multiple_of(i * step, step), step)
            term_kv[at] = lax.dot_general(
                hidden_ref[:, at], grad_kv_ref[...], (((0,), (0,)), ((), ())),
                preferred_element_type=jnp.float32,
            ).astype(jnp.bfloat16)
            return carry

        lax.fori_loop(0, term_kv.shape[0] // step, body, 0)
        for p in late:
            launch(p)

    lag = 2
    sends, latest = ([], {})
    for turn in range(stages + 1 + lag):
        if turn == lag:
            own_keys()
        for p, (index, start, width, order) in enumerate(parts):
            stage = turn - lag if p in late else turn
            if stage < 0 or stage > stages:
                continue
            size = half_rows >> stage
            if stage == 0:
                whole = terms[index].at[pl.ds(0, half_rows), pl.ds(start, width)]
                pltpu.make_async_copy(whole, accs[p][0], own_sem.at[p]).wait()
                copy = pltpu.make_async_remote_copy(
                    src_ref=whole, dst_ref=recvs[p][0],
                    send_sem=send_sem.at[p, 0], recv_sem=recv_sem.at[p, 0],
                    device_id=partner(core), device_id_type=MESH,
                )
                copy.wait_recv()
                sends.append(copy)
                target, base, source = (accs[p][0], 0, accs[p][0])
            else:
                bit = orders[order][stage - 1]
                latest[p].wait_recv()
                source = accs[p][stage - 1]
                base = my_bit(bit) * size
                target = accs[p][stage] if stage < stages else out_ref
            last = pl.ds(offsets[index] + start, width) if stage == stages else None
            add(target, source, base, recvs[p][stage], size, last)
            if stage < stages:
                bit = orders[order][stage]
                send_from = pl.multiple_of((1 - my_bit(bit)) * (size // 2), size // 2)
                copy = pltpu.make_async_remote_copy(
                    src_ref=target.at[pl.ds(send_from, size // 2)],
                    dst_ref=recvs[p][stage + 1],
                    send_sem=send_sem.at[p, stage + 1], recv_sem=recv_sem.at[p, stage + 1],
                    device_id=partner(bit), device_id_type=MESH,
                )
                copy.start()
                latest[p] = copy
                sends.append(copy)
    for copy in sends:
        copy.wait_send()
    for hop in range(1, preds + 1):

        @pl.when(ctx_at >= hop)
        def _():
            piece_copy(hop, ctx_at - hop).wait_send()


def reduce_terms(term_q, term_o, hidden, pieces, scale):
    ctx_count, fsdp_count = (lax.axis_size("ctx"), lax.axis_size("fsdp"))
    preds = len(pieces) - 1
    widths = [term_q.shape[1], pieces[0].shape[1], term_o.shape[1]]
    parts = reduce_parts(widths)
    count = ctx_count * fsdp_count
    block = term_q.shape[0] // count
    stages = count.bit_length() - 2
    scratch = [
        pltpu.VMEM((preds,) + pieces[0].shape, jnp.bfloat16),
        pltpu.VMEM(pieces[0].shape, jnp.float32),
        pltpu.VMEM((term_q.shape[0], widths[1]), jnp.bfloat16),
        pltpu.SemaphoreType.DMA((preds,)),
        pltpu.SemaphoreType.DMA((preds,)),
    ]
    for _, _, width, _ in parts:
        half_rows = count // 2 * block
        for stage in range(stages):
            scratch.append(pltpu.VMEM((half_rows >> stage, width), jnp.bfloat16))
        for stage in range(stages + 1):
            scratch.append(pltpu.VMEM((half_rows >> stage, width), jnp.bfloat16))
    scratch += [
        pltpu.SemaphoreType.DMA((len(parts),)),
        pltpu.SemaphoreType.DMA((len(parts), stages + 1)),
        pltpu.SemaphoreType.DMA((len(parts), stages + 1)),
    ]
    return pl.pallas_call(
        functools.partial(reduce_kernel, ctx_count, fsdp_count, preds, parts, scale),
        out_shape=[
            jax.ShapeDtypeStruct((block, sum(widths)), jnp.float32),
            jax.ShapeDtypeStruct(pieces[0].shape, jnp.bfloat16),
        ],
        in_specs=[pl.BlockSpec(memory_space=pl.ANY)] * 2
        + [pl.BlockSpec(memory_space=pltpu.VMEM)] * (preds + 2),
        out_specs=[pl.BlockSpec(memory_space=pltpu.VMEM)] * 2,
        scratch_shapes=scratch,
        compiler_params=pltpu.CompilerParams(
            collective_id=1, has_side_effects=True, vmem_limit_bytes=40 * 1024 * 1024
        ),
        name="reduce_terms",
    )(term_q, term_o, hidden, *pieces)


def from_behind(value, axis, steps):
    count = lax.axis_size(axis)
    leading, last = (max(0, -steps), min(count, count - steps))
    return lax.ppermute(value, axis, [(source, source + steps) for source in range(leading, last)])


def normalize(rows):
    values = rows.astype(jnp.float32)
    inv_rms = lax.rsqrt(jnp.mean(values * values, axis=-1, keepdims=True) + EPS)
    return (values * inv_rms, inv_rms)


def attend_kernel(preds, q_ref, g_ref, *refs):
    count = preds + 1
    keys, values, refs = (refs[:count], refs[count : 2 * count], refs[2 * count :])
    attended_ref, dq_ref, dkv_refs, refs = (refs[0], refs[1], refs[2 : 2 + count], refs[2 + count :])
    bias, work, dk_acc, dv_acc = refs
    shard = q_ref.shape[0]
    group = pl.program_id(0)
    heads = q_ref.shape[1] // HEAD_SIZE
    scale = 1.0 / math.sqrt(HEAD_SIZE)
    contract_last = (((1,), (1,)), ((), ()))
    contract_mid = (((1,), (0,)), ((), ()))

    def dot(a, b, dims):
        return lax.dot_general(a, b, dims, preferred_element_type=jnp.float32)

    @pl.when(group == 0)
    def _():
        base = lax.axis_index("ctx") * shard
        key_at = lax.broadcasted_iota(jnp.int32, (shard, shard), 0)
        query_at = lax.broadcasted_iota(jnp.int32, (shard, shard), 1)
        for block in range(count):
            key_pos = key_at + (block - preds) * shard
            offset = query_at - key_pos
            allowed = (offset >= 0) & (offset < WINDOW_TOKENS) & (key_pos + base >= 0)
            bias[block] = jnp.where(allowed, 0.0, -jnp.inf)

    keys_t = [k[...].T for k in keys]
    values_t = [v[...].T for v in values]
    for head in range(heads):
        columns = slice(head * HEAD_SIZE, (head + 1) * HEAD_SIZE)
        q = q_ref[:, columns]
        g = g_ref[:, columns]
        slot = head % 2
        top = None
        for block in range(count):
            scores = dot(keys[block][...], q, contract_last) * (scale * math.log2(math.e))
            scores = scores + bias[block]
            work[slot, block] = scores
            peak = jnp.max(scores, axis=0, keepdims=True)
            top = peak if top is None else jnp.maximum(top, peak)
        total = 0.0
        for block in range(count):
            expo = jnp.exp2(work[slot, block] - top)
            work[slot, block] = expo
            total = total + jnp.sum(expo, axis=0, keepdims=True)
        inverse = 1.0 / total
        attended_t = 0.0
        for block in range(count):
            probs = work[slot, block] * inverse
            work[slot, block] = probs
            probs_low = probs.astype(jnp.bfloat16)
            attended_t = attended_t + dot(values_t[block], probs_low, contract_mid)
            dv = dot(probs_low, g, contract_mid)
            dv_acc[block] = dv if head == 0 else dv_acc[block] + dv
        delta = jnp.sum(g.astype(jnp.float32).T * attended_t, axis=0, keepdims=True)
        attended_ref[:, columns] = attended_t.T.astype(jnp.bfloat16)
        dq_t = 0.0
        for block in range(count):
            grad_probs = dot(values[block][...], g, contract_last)
            grad_scores = work[slot, block] * (grad_probs - delta) * scale
            grad_scores = grad_scores.astype(jnp.bfloat16)
            dq_t = dq_t + dot(keys_t[block], grad_scores, contract_mid)
            dk = dot(grad_scores, q, contract_mid)
            dk_acc[block] = dk if head == 0 else dk_acc[block] + dk
        dq_ref[:, columns] = dq_t.T.astype(jnp.bfloat16)
    for block in range(count):
        at = pl.multiple_of(group * HEAD_SIZE, HEAD_SIZE)
        dkv_refs[block][:, pl.ds(at, HEAD_SIZE)] = dk_acc[block].astype(jnp.bfloat16)
        at = pl.multiple_of((KEY_VALUE_HEADS + group) * HEAD_SIZE, HEAD_SIZE)
        dkv_refs[block][:, pl.ds(at, HEAD_SIZE)] = dv_acc[block].astype(jnp.bfloat16)


def attend(query_rows, grad_rows, blocks):
    shard, width = query_rows.shape
    count = len(blocks)
    group_width = width // KEY_VALUE_HEADS
    query_spec = pl.BlockSpec((shard, group_width), lambda i: (0, i))
    key_spec = pl.BlockSpec((shard, HEAD_SIZE), lambda i: (0, i))
    value_spec = pl.BlockSpec((shard, HEAD_SIZE), lambda i: (0, KEY_VALUE_HEADS + i))
    pair_spec = pl.BlockSpec((shard, blocks[0].shape[1]), lambda i: (0, 0))
    wide = jax.ShapeDtypeStruct((shard, width), jnp.bfloat16)
    pair = jax.ShapeDtypeStruct(blocks[0].shape, jnp.bfloat16)
    flops = 10 * shard * shard * count * width
    return pl.pallas_call(
        functools.partial(attend_kernel, count - 1),
        grid=(KEY_VALUE_HEADS,),
        out_shape=[wide, wide] + [pair] * count,
        in_specs=[query_spec] * 2 + [key_spec] * count + [value_spec] * count,
        out_specs=[query_spec] * 2 + [pair_spec] * count,
        scratch_shapes=[
            pltpu.VMEM((count, shard, shard), jnp.float32),
            pltpu.VMEM((2, count, shard, shard), jnp.float32),
            pltpu.VMEM((count, shard, HEAD_SIZE), jnp.float32),
            pltpu.VMEM((count, shard, HEAD_SIZE), jnp.float32),
        ],
        compiler_params=pltpu.CompilerParams(vmem_limit_bytes=40 * 1024 * 1024),
        cost_estimate=pl.CostEstimate(
            flops=flops, bytes_accessed=4 * 1024 * 1024, transcendentals=shard * shard * count * 8
        ),
        name="attend",
    )(query_rows, grad_rows, *blocks, *blocks)


def shards(x_cur, x_next, cot_cur, cot_next, w_q, w_kv, w_out):
    full_q, full_kv, full_out = gather_weights(w_q, w_kv, w_out)
    seq_count, shard, width = x_cur.shape
    preds = WINDOW_TOKENS // shard
    normed, inv_rms = normalize(x_cur)
    hidden = normed.astype(jnp.bfloat16)
    query_rows = jnp.einsum(
        "sid,dc->sic", hidden, full_q, preferred_element_type=jnp.float32
    ).astype(jnp.bfloat16)
    key_value_pairs = jnp.einsum(
        "sid,dc->sic", hidden, full_kv, preferred_element_type=jnp.float32
    ).astype(jnp.bfloat16)
    grad_attn = (
        2.0 * jnp.einsum("sid,dc->sic", cot_next, full_out, preferred_element_type=jnp.float32)
    ).astype(jnp.bfloat16)
    earlier = []
    for hop in range(1, preds + 1):
        earlier.append(from_behind(key_value_pairs, "ctx", hop))
    results = []
    for seq in range(seq_count):
        window = [block[seq] for block in earlier[::-1]] + [key_value_pairs[seq]]
        results.append(attend(query_rows[seq], grad_attn[seq], window))
    attended, grad_query, *pieces = (jnp.stack(parts) for parts in zip(*results))
    layer_out = jnp.einsum("sic,dc->sid", attended, full_out, preferred_element_type=jnp.float32)
    x_prev = (x_next.astype(jnp.float32) - 2.0 * layer_out).astype(jnp.bfloat16)
    hidden_rows = hidden.reshape(seq_count * shard, width)
    cot_rows = cot_next.reshape(seq_count * shard, width)
    query_left = grad_query.reshape(seq_count * shard, -1)
    attended_rows = attended.reshape(seq_count * shard, -1)
    contract_rows = (((0,), (0,)), ((), ()))
    ctx_count = lax.axis_size("ctx")
    fsdp_count = lax.axis_size("fsdp")
    term_q = lax.dot_general(
        hidden_rows, query_left, contract_rows, preferred_element_type=jnp.float32
    )
    term_out = 2.0 * lax.dot_general(
        cot_rows, attended_rows, contract_rows, preferred_element_type=jnp.float32
    )
    token_total = seq_count * shard * ctx_count * fsdp_count
    grad_weights, grad_kv = reduce_terms(
        term_q.astype(jnp.bfloat16),
        term_out.astype(jnp.bfloat16),
        hidden_rows,
        [piece.reshape(seq_count * shard, -1) for piece in pieces],
        1.0 / math.sqrt(token_total),
    )
    grad_kv = grad_kv.reshape(seq_count, shard, -1)
    grad_hidden = jnp.einsum("sic,dc->sid", grad_query, full_q, preferred_element_type=jnp.float32)
    grad_hidden = grad_hidden + jnp.einsum(
        "sic,dc->sid", grad_kv, full_kv, preferred_element_type=jnp.float32
    )
    grad_x = inv_rms * (
        grad_hidden - normed * jnp.mean(grad_hidden * normed, axis=-1, keepdims=True)
    )
    grad_cur = (cot_cur.astype(jnp.float32) + grad_x).astype(jnp.bfloat16)
    return (x_prev, grad_cur, grad_weights)


def solution(mesh):
    in_specs = (
        P("fsdp", "ctx", None),
        P("fsdp", "ctx", None),
        P("fsdp", "ctx", None),
        P("fsdp", "ctx", None),
        P("fsdp", None),
        P("fsdp", None),
        P("fsdp", None),
    )
    out_specs = (P("fsdp", "ctx", None), P("fsdp", "ctx", None), P(("ctx", "fsdp"), None))
    return jax.shard_map(shards, mesh=mesh, in_specs=in_specs, out_specs=out_specs, check_vma=False)
```

```python
import functools
import math

import jax
import jax.numpy as jnp
from jax import lax
from jax.experimental import pallas as pl
from jax.experimental.pallas import tpu as pltpu
from jax.sharding import PartitionSpec as P

QUERY_HEADS = 8
KEY_VALUE_HEADS = 2
HEAD_SIZE = 128
WINDOW_TOKENS = 1024


EPS = 1e-05


MESH = pl.DeviceIdType.MESH


def gather_kernel(fsdp_count, q_in, kv_in, o_in, q_out, kv_out, o_out, own_sem, send_sem, recv_sem):
    ctx_at = lax.axis_index("ctx")
    fsdp_at = lax.axis_index("fsdp")
    half_at = lax.rem(ctx_at, 2)
    side = ctx_at + 1 - 2 * half_at
    core = fsdp_at + 1 - 2 * lax.rem(fsdp_at, 2)
    across = lax.rem(fsdp_at + fsdp_count // 2, fsdp_count)
    across_core = lax.rem(core + fsdp_count // 2, fsdp_count)
    ins, outs = ((q_in, kv_in, o_in), (q_out, kv_out, o_out))
    rows = q_in.shape[0]
    half = rows // 2
    pieces = []
    for index in (1, 0, 2):
        cuts = 1 if index == 1 else 2
        for cut in range(cuts):
            pieces.append((index, cut * (half // cuts), half // cuts))
    count = len(pieces)

    barrier = pltpu.get_barrier_semaphore()
    for target in ((ctx_at, core), (ctx_at, across), (side, fsdp_at)):
        pl.semaphore_signal(barrier, inc=1, device_id=target, device_id_type=MESH)
    pl.semaphore_wait(barrier, 3)

    def at(ref, owner, which, piece):
        _, start, size = piece
        return ref.at[pl.ds(pl.multiple_of(owner * rows + which * half + start, 128), size)]

    def remote(src, dst, slot, target):
        return pltpu.make_async_remote_copy(
            src_ref=src, dst_ref=dst, send_sem=send_sem.at[slot], recv_sem=recv_sem.at[slot],
            device_id=target, device_id_type=MESH,
        )

    y_copies = []
    for i, piece in enumerate(pieces):
        index, start, size = piece
        copy = remote(
            ins[index].at[pl.ds(pl.multiple_of(half_at * half + start, 128), size)],
            at(outs[index], fsdp_at, half_at, piece), i, (ctx_at, across),
        )
        copy.start()
        y_copies.append(copy)
    own_copies, core_copies = ([], [])
    for index in (1, 0, 2):
        place = outs[index].at[pl.ds(pl.multiple_of(fsdp_at * rows, 128), rows)]
        copy = remote(ins[index], place, 4 * count + index, (ctx_at, core))
        copy.start()
        core_copies.append(copy)
        copy = pltpu.make_async_copy(ins[index], place, own_sem.at[index])
        copy.start()
        own_copies.append(copy)
    x_copies = []
    for i, piece in enumerate(pieces):
        out = outs[piece[0]]
        here = at(out, across, half_at, piece)
        remote(here, here, i, (ctx_at, across)).wait_recv()
        copy = remote(here, here, count + i, (side, fsdp_at))
        copy.start()
        x_copies.append(copy)
        copy = remote(here, here, 2 * count + i, (ctx_at, core))
        copy.start()
        core_copies.append(copy)
    for i, piece in enumerate(pieces):
        here = at(outs[piece[0]], across, 1 - half_at, piece)
        remote(here, here, count + i, (side, fsdp_at)).wait_recv()
        copy = remote(here, here, 3 * count + i, (ctx_at, core))
        copy.start()
        core_copies.append(copy)
    for i, piece in enumerate(pieces):
        for level, which in ((2, half_at), (3, 1 - half_at)):
            here = at(outs[piece[0]], across_core, which, piece)
            remote(here, here, level * count + i, (ctx_at, core)).wait_recv()
    for index in range(3):
        place = outs[index].at[pl.ds(pl.multiple_of(core * rows, 128), rows)]
        remote(ins[index], place, 4 * count + index, (ctx_at, core)).wait_recv()
    for copy in y_copies + x_copies + core_copies:
        copy.wait_send()
    for copy in own_copies:
        copy.wait()


def gather_weights(w_q, w_kv, w_out):
    count = lax.axis_size("fsdp")
    shapes = [
        jax.ShapeDtypeStruct((count * w.shape[0], w.shape[1]), w.dtype) for w in (w_q, w_kv, w_out)
    ]
    slots = 4 * 5 + 3
    return pl.pallas_call(
        functools.partial(gather_kernel, count),
        out_shape=shapes,
        in_specs=[pl.BlockSpec(memory_space=pl.ANY)] * 3,
        out_specs=[pl.BlockSpec(memory_space=pltpu.VMEM)] * 3,
        scratch_shapes=[
            pltpu.SemaphoreType.DMA((3,)),
            pltpu.SemaphoreType.DMA((slots,)),
            pltpu.SemaphoreType.DMA((slots,)),
        ],
        compiler_params=pltpu.CompilerParams(
            collective_id=0, has_side_effects=True, vmem_limit_bytes=40 * 1024 * 1024
        ),
        name="gather_weights",
    )(w_q, w_kv, w_out)


def reduce_plan(ctx_count, fsdp_count):
    ctx_bits = [("ctx", 1 << i) for i in range(ctx_count.bit_length() - 1)]
    fsdp_bits = [("fsdp", 1 << i) for i in range(fsdp_count.bit_length() - 1)]
    core, rest = (fsdp_bits[0], fsdp_bits[1:])
    order_a = rest + ctx_bits
    order_b = ctx_bits + rest
    order_c = ctx_bits[1:2] + rest + ctx_bits[:1] + ctx_bits[2:]
    return core, order_a, order_b, order_c


def reduce_parts(widths):
    q_width, kv_width, o_width = widths
    tail = 256
    half = kv_width // 2
    return (
        (0, 0, q_width - tail, 0),
        (2, 0, o_width - tail, 1),
        (0, q_width - tail, tail, 2),
        (2, o_width - tail, tail, 2),
        (1, 0, half, 0),
        (1, half, half, 1),
    )


def reduce_kernel(ctx_count, fsdp_count, preds, parts, scale, *refs):
    term_q, term_o, hidden_ref, refs = (refs[0], refs[1], refs[2], refs[3:])
    pieces, out_ref, grad_kv_ref, refs = (refs[: preds + 1], refs[preds + 1], refs[preds + 2], refs[preds + 3 :])
    arrived, kv_sum, term_kv, kv_send, kv_recv = refs[:5]
    refs = refs[5:]
    terms = (term_q, term_kv, term_o)
    core, *orders = reduce_plan(ctx_count, fsdp_count)
    stages = len(orders[0])
    accs, recvs = ([], [])
    for _ in parts:
        accs.append(refs[: stages])
        recvs.append(refs[stages : 2 * stages + 1])
        refs = refs[2 * stages + 1 :]
    own_sem, send_sem, recv_sem = refs
    place = {"ctx": lax.axis_index("ctx"), "fsdp": lax.axis_index("fsdp")}
    count = ctx_count * fsdp_count
    block = terms[0].shape[0] // count
    offsets = (0, terms[0].shape[1], terms[0].shape[1] + terms[1].shape[1])

    def my_bit(bit):
        return lax.rem(place[bit[0]] // bit[1], 2)

    def partner(bit):
        flipped = place[bit[0]] + bit[1] * (1 - 2 * my_bit(bit))
        return (flipped, place["fsdp"]) if bit[0] == "ctx" else (place["ctx"], flipped)

    barrier = pltpu.get_barrier_semaphore()
    for bit in [core] + orders[0]:
        pl.semaphore_signal(barrier, inc=1, device_id=partner(bit), device_id_type=MESH)
    ctx_at = place["ctx"]
    for hop in range(1, preds + 1):

        @pl.when(ctx_at + hop < ctx_count)
        def _():
            pl.semaphore_signal(
                barrier, inc=1, device_id=(ctx_at + hop, place["fsdp"]), device_id_type=MESH
            )

    pl.semaphore_wait(barrier, stages + 1 + jnp.minimum(ctx_at, preds))

    def piece_copy(hop, target):
        return pltpu.make_async_remote_copy(
            src_ref=pieces[preds - hop], dst_ref=arrived.at[hop - 1],
            send_sem=kv_send.at[hop - 1], recv_sem=kv_recv.at[hop - 1],
            device_id=(target, place["fsdp"]), device_id_type=MESH,
        )

    for hop in range(1, preds + 1):

        @pl.when(ctx_at >= hop)
        def _():
            piece_copy(hop, ctx_at - hop).start()

    half_blocks = count // 2

    def launch(p):
        index, start, width, order = parts[p]
        columns = pl.ds(start, width)

        def one(j, carry):
            owner = 0
            for i, bit in enumerate(orders[order]):
                digit = lax.rem(j // (half_blocks >> (i + 1)), 2)
                owner = owner + digit * bit[1] * (fsdp_count if bit[0] == "ctx" else 1)
            slot = pl.ds(pl.multiple_of(j * block, block), block)

            def rows(core_bit):
                return pl.ds(pl.multiple_of((owner + core_bit * core[1]) * block, block), block)

            pltpu.make_async_remote_copy(
                src_ref=terms[index].at[rows(1 - my_bit(core)), columns],
                dst_ref=recvs[p][0].at[slot],
                send_sem=send_sem.at[p, 0], recv_sem=recv_sem.at[p, 0],
                device_id=partner(core), device_id_type=MESH,
            ).start()
            pltpu.make_async_copy(
                terms[index].at[rows(my_bit(core)), columns], accs[p][0].at[slot], own_sem.at[p]
            ).start()
            return carry

        lax.fori_loop(0, half_blocks, one, 0)

    def add(target, first, base, second, size, last):
        step = min(size, 64)

        def body(i, carry):
            at = pl.multiple_of(i * step, step)
            value = first[pl.ds(pl.multiple_of(base + at, step), step)].astype(jnp.float32)
            value = value + second[pl.ds(at, step)].astype(jnp.float32)
            if last is None:
                target[pl.ds(at, step)] = value.astype(target.dtype)
            else:
                target[pl.ds(at, step), last] = value * scale
            return carry

        lax.fori_loop(0, size // step, body, 0)

    half_rows = half_blocks * block
    early = [p for p, part in enumerate(parts) if part[0] != 1]
    late = [p for p, part in enumerate(parts) if part[0] == 1]
    for p in early:
        launch(p)

    def own_keys():
        kv_sum[...] = pieces[preds][...].astype(jnp.float32)
        for hop in range(1, preds + 1):

            @pl.when(ctx_at + hop < ctx_count)
            def _():
                piece_copy(hop, ctx_at + hop).wait_recv()
                kv_sum[...] += arrived[hop - 1].astype(jnp.float32)

        grad_kv_ref[...] = kv_sum[...].astype(jnp.bfloat16)
        step = 256

        def body(i, carry):
            at = pl.ds(pl.multiple_of(i * step, step), step)
            term_kv[at] = lax.dot_general(
                hidden_ref[:, at], grad_kv_ref[...], (((0,), (0,)), ((), ())),
                preferred_element_type=jnp.float32,
            ).astype(jnp.bfloat16)
            return carry

        lax.fori_loop(0, term_kv.shape[0] // step, body, 0)
        for p in late:
            launch(p)

    lag = 2
    sends, latest = ([], {})
    for turn in range(stages + 1 + lag):
        if turn == lag:
            own_keys()
        for p, (index, start, width, order) in enumerate(parts):
            stage = turn - lag if p in late else turn
            if stage < 0 or stage > stages:
                continue
            size = half_rows >> stage
            if stage == 0:
                whole = terms[index].at[pl.ds(0, half_rows), pl.ds(start, width)]
                pltpu.make_async_copy(whole, accs[p][0], own_sem.at[p]).wait()
                copy = pltpu.make_async_remote_copy(
                    src_ref=whole, dst_ref=recvs[p][0],
                    send_sem=send_sem.at[p, 0], recv_sem=recv_sem.at[p, 0],
                    device_id=partner(core), device_id_type=MESH,
                )
                copy.wait_recv()
                sends.append(copy)
                target, base, source = (accs[p][0], 0, accs[p][0])
            else:
                bit = orders[order][stage - 1]
                latest[p].wait_recv()
                source = accs[p][stage - 1]
                base = my_bit(bit) * size
                target = accs[p][stage] if stage < stages else out_ref
            last = pl.ds(offsets[index] + start, width) if stage == stages else None
            add(target, source, base, recvs[p][stage], size, last)
            if stage < stages:
                bit = orders[order][stage]
                send_from = pl.multiple_of((1 - my_bit(bit)) * (size // 2), size // 2)
                copy = pltpu.make_async_remote_copy(
                    src_ref=target.at[pl.ds(send_from, size // 2)],
                    dst_ref=recvs[p][stage + 1],
                    send_sem=send_sem.at[p, stage + 1], recv_sem=recv_sem.at[p, stage + 1],
                    device_id=partner(bit), device_id_type=MESH,
                )
                copy.start()
                latest[p] = copy
                sends.append(copy)
    for copy in sends:
        copy.wait_send()
    for hop in range(1, preds + 1):

        @pl.when(ctx_at >= hop)
        def _():
            piece_copy(hop, ctx_at - hop).wait_send()


def reduce_terms(term_q, term_o, hidden, pieces, scale):
    ctx_count, fsdp_count = (lax.axis_size("ctx"), lax.axis_size("fsdp"))
    preds = len(pieces) - 1
    widths = [term_q.shape[1], pieces[0].shape[1], term_o.shape[1]]
    parts = reduce_parts(widths)
    count = ctx_count * fsdp_count
    block = term_q.shape[0] // count
    stages = count.bit_length() - 2
    scratch = [
        pltpu.VMEM((preds,) + pieces[0].shape, jnp.bfloat16),
        pltpu.VMEM(pieces[0].shape, jnp.float32),
        pltpu.VMEM((term_q.shape[0], widths[1]), jnp.bfloat16),
        pltpu.SemaphoreType.DMA((preds,)),
        pltpu.SemaphoreType.DMA((preds,)),
    ]
    for _, _, width, _ in parts:
        half_rows = count // 2 * block
        for stage in range(stages):
            scratch.append(pltpu.VMEM((half_rows >> stage, width), jnp.bfloat16))
        for stage in range(stages + 1):
            scratch.append(pltpu.VMEM((half_rows >> stage, width), jnp.bfloat16))
    scratch += [
        pltpu.SemaphoreType.DMA((len(parts),)),
        pltpu.SemaphoreType.DMA((len(parts), stages + 1)),
        pltpu.SemaphoreType.DMA((len(parts), stages + 1)),
    ]
    return pl.pallas_call(
        functools.partial(reduce_kernel, ctx_count, fsdp_count, preds, parts, scale),
        out_shape=[
            jax.ShapeDtypeStruct((block, sum(widths)), jnp.float32),
            jax.ShapeDtypeStruct(pieces[0].shape, jnp.bfloat16),
        ],
        in_specs=[pl.BlockSpec(memory_space=pl.ANY)] * 2
        + [pl.BlockSpec(memory_space=pltpu.VMEM)] * (preds + 2),
        out_specs=[pl.BlockSpec(memory_space=pltpu.VMEM)] * 2,
        scratch_shapes=scratch,
        compiler_params=pltpu.CompilerParams(
            collective_id=1, has_side_effects=True, vmem_limit_bytes=40 * 1024 * 1024
        ),
        name="reduce_terms",
    )(term_q, term_o, hidden, *pieces)


def share_kernel(ctx_count, kv_ref, hop1, hop2, hop3, hop4, send_sem, recv_sem):
    ctx_at = lax.axis_index("ctx")
    fsdp_at = lax.axis_index("fsdp")
    odd = lax.rem(ctx_at, 2)
    peer = ctx_at + 1 - 2 * odd
    slots = (hop1, hop2, hop3, hop4)

    barrier = pltpu.get_barrier_semaphore()
    pl.semaphore_signal(barrier, inc=1, device_id=(peer, fsdp_at), device_id_type=MESH)

    @pl.when(ctx_at >= 2)
    def _():
        pl.semaphore_signal(barrier, inc=1, device_id=(ctx_at - 2, fsdp_at), device_id_type=MESH)

    pl.semaphore_wait(barrier, 1 + jnp.minimum((ctx_count - 1 - ctx_at) // 2, 1))

    def copy(src, hop, slot, target):
        return pltpu.make_async_remote_copy(
            src_ref=src, dst_ref=slots[hop - 1],
            send_sem=send_sem.at[slot], recv_sem=recv_sem.at[hop - 1],
            device_id=(target, fsdp_at), device_id_type=MESH,
        )

    onward = ctx_at + 2 < ctx_count
    plan = (
        (onward, kv_ref, 2, 0, ctx_at + 2),
        (odd == 0, kv_ref, 1, 1, peer),
        ((ctx_at >= 2) & onward, hop2, 4, 2, ctx_at + 2),
        ((ctx_at >= 2) & (odd == 0), hop2, 3, 3, peer),
        ((ctx_at >= 2) & (odd == 1), hop2, 1, 4, peer),
        ((ctx_at >= 4) & (odd == 1), hop4, 3, 5, peer),
    )

    def begin(entries):
        for valid, src, hop, slot, target in entries:

            @pl.when(valid)
            def _():
                copy(src, hop, slot, target).start()

    def arrive(hop):
        @pl.when(ctx_at >= hop)
        def _():
            copy(kv_ref, hop, 0, peer).wait_recv()

    begin(plan[:2])
    for hop in range(1, 5):

        @pl.when(ctx_at < hop)
        def _():
            slots[hop - 1][...] = jnp.zeros_like(slots[hop - 1])

    arrive(2)
    begin(plan[2:5])
    arrive(4)
    begin(plan[5:])
    arrive(1)
    arrive(3)
    for valid, src, hop, slot, target in plan:

        @pl.when(valid)
        def _():
            copy(src, hop, slot, target).wait_send()


def share_keys(rows):
    return pl.pallas_call(
        functools.partial(share_kernel, lax.axis_size("ctx")),
        out_shape=[jax.ShapeDtypeStruct(rows.shape, rows.dtype)] * 4,
        in_specs=[pl.BlockSpec(memory_space=pltpu.VMEM)],
        out_specs=[pl.BlockSpec(memory_space=pltpu.VMEM)] * 4,
        scratch_shapes=[pltpu.SemaphoreType.DMA((6,)), pltpu.SemaphoreType.DMA((4,))],
        compiler_params=pltpu.CompilerParams(collective_id=2, has_side_effects=True),
        name="share_keys",
    )(rows)


def from_behind(value, axis, steps):
    count = lax.axis_size(axis)
    leading, last = (max(0, -steps), min(count, count - steps))
    return lax.ppermute(value, axis, [(source, source + steps) for source in range(leading, last)])


def normalize(rows):
    values = rows.astype(jnp.float32)
    inv_rms = lax.rsqrt(jnp.mean(values * values, axis=-1, keepdims=True) + EPS)
    return (values * inv_rms, inv_rms)


def attend_kernel(preds, q_ref, g_ref, *refs):
    count = preds + 1
    keys, values, refs = (refs[:count], refs[count : 2 * count], refs[2 * count :])
    attended_ref, dq_ref, dkv_refs, refs = (refs[0], refs[1], refs[2 : 2 + count], refs[2 + count :])
    bias, work, dk_acc, dv_acc = refs
    shard = q_ref.shape[0]
    group = pl.program_id(0)
    heads = q_ref.shape[1] // HEAD_SIZE
    scale = 1.0 / math.sqrt(HEAD_SIZE)
    contract_last = (((1,), (1,)), ((), ()))
    contract_mid = (((1,), (0,)), ((), ()))

    def dot(a, b, dims):
        return lax.dot_general(a, b, dims, preferred_element_type=jnp.float32)

    @pl.when(group == 0)
    def _():
        base = lax.axis_index("ctx") * shard
        key_at = lax.broadcasted_iota(jnp.int32, (shard, shard), 0)
        query_at = lax.broadcasted_iota(jnp.int32, (shard, shard), 1)
        for block in range(count):
            key_pos = key_at + (block - preds) * shard
            offset = query_at - key_pos
            allowed = (offset >= 0) & (offset < WINDOW_TOKENS) & (key_pos + base >= 0)
            bias[block] = jnp.where(allowed, 0.0, -jnp.inf)

    keys_t = [k[...].T for k in keys]
    values_t = [v[...].T for v in values]
    for head in range(heads):
        columns = slice(head * HEAD_SIZE, (head + 1) * HEAD_SIZE)
        q = q_ref[:, columns]
        g = g_ref[:, columns]
        slot = head % 2
        top = None
        for block in range(count):
            scores = dot(keys[block][...], q, contract_last) * (scale * math.log2(math.e))
            scores = scores + bias[block]
            work[slot, block] = scores
            peak = jnp.max(scores, axis=0, keepdims=True)
            top = peak if top is None else jnp.maximum(top, peak)
        total = 0.0
        for block in range(count):
            expo = jnp.exp2(work[slot, block] - top)
            work[slot, block] = expo
            total = total + jnp.sum(expo, axis=0, keepdims=True)
        inverse = 1.0 / total
        attended_t = 0.0
        for block in range(count):
            probs = work[slot, block] * inverse
            work[slot, block] = probs
            probs_low = probs.astype(jnp.bfloat16)
            attended_t = attended_t + dot(values_t[block], probs_low, contract_mid)
            dv = dot(probs_low, g, contract_mid)
            dv_acc[block] = dv if head == 0 else dv_acc[block] + dv
        delta = jnp.sum(g.astype(jnp.float32).T * attended_t, axis=0, keepdims=True)
        attended_ref[:, columns] = attended_t.T.astype(jnp.bfloat16)
        dq_t = 0.0
        for block in range(count):
            grad_probs = dot(values[block][...], g, contract_last)
            grad_scores = work[slot, block] * (grad_probs - delta) * scale
            grad_scores = grad_scores.astype(jnp.bfloat16)
            dq_t = dq_t + dot(keys_t[block], grad_scores, contract_mid)
            dk = dot(grad_scores, q, contract_mid)
            dk_acc[block] = dk if head == 0 else dk_acc[block] + dk
        dq_ref[:, columns] = dq_t.T.astype(jnp.bfloat16)
    for block in range(count):
        at = pl.multiple_of(group * HEAD_SIZE, HEAD_SIZE)
        dkv_refs[block][:, pl.ds(at, HEAD_SIZE)] = dk_acc[block].astype(jnp.bfloat16)
        at = pl.multiple_of((KEY_VALUE_HEADS + group) * HEAD_SIZE, HEAD_SIZE)
        dkv_refs[block][:, pl.ds(at, HEAD_SIZE)] = dv_acc[block].astype(jnp.bfloat16)


def attend(query_rows, grad_rows, blocks):
    shard, width = query_rows.shape
    count = len(blocks)
    group_width = width // KEY_VALUE_HEADS
    query_spec = pl.BlockSpec((shard, group_width), lambda i: (0, i))
    key_spec = pl.BlockSpec((shard, HEAD_SIZE), lambda i: (0, i))
    value_spec = pl.BlockSpec((shard, HEAD_SIZE), lambda i: (0, KEY_VALUE_HEADS + i))
    pair_spec = pl.BlockSpec((shard, blocks[0].shape[1]), lambda i: (0, 0))
    wide = jax.ShapeDtypeStruct((shard, width), jnp.bfloat16)
    pair = jax.ShapeDtypeStruct(blocks[0].shape, jnp.bfloat16)
    flops = 10 * shard * shard * count * width
    return pl.pallas_call(
        functools.partial(attend_kernel, count - 1),
        grid=(KEY_VALUE_HEADS,),
        out_shape=[wide, wide] + [pair] * count,
        in_specs=[query_spec] * 2 + [key_spec] * count + [value_spec] * count,
        out_specs=[query_spec] * 2 + [pair_spec] * count,
        scratch_shapes=[
            pltpu.VMEM((count, shard, shard), jnp.float32),
            pltpu.VMEM((2, count, shard, shard), jnp.float32),
            pltpu.VMEM((count, shard, HEAD_SIZE), jnp.float32),
            pltpu.VMEM((count, shard, HEAD_SIZE), jnp.float32),
        ],
        compiler_params=pltpu.CompilerParams(vmem_limit_bytes=40 * 1024 * 1024),
        cost_estimate=pl.CostEstimate(
            flops=flops, bytes_accessed=4 * 1024 * 1024, transcendentals=shard * shard * count * 8
        ),
        name="attend",
    )(query_rows, grad_rows, *blocks, *blocks)


def shards(x_cur, x_next, cot_cur, cot_next, w_q, w_kv, w_out):
    full_q, full_kv, full_out = gather_weights(w_q, w_kv, w_out)
    seq_count, shard, width = x_cur.shape
    preds = WINDOW_TOKENS // shard
    normed, inv_rms = normalize(x_cur)
    hidden = normed.astype(jnp.bfloat16)
    query_rows = jnp.einsum(
        "sid,dc->sic", hidden, full_q, preferred_element_type=jnp.float32
    ).astype(jnp.bfloat16)
    key_value_pairs = jnp.einsum(
        "sid,dc->sic", hidden, full_kv, preferred_element_type=jnp.float32
    ).astype(jnp.bfloat16)
    grad_attn = (
        2.0 * jnp.einsum("sid,dc->sic", cot_next, full_out, preferred_element_type=jnp.float32)
    ).astype(jnp.bfloat16)
    if preds == 4 and lax.axis_size("ctx") % 2 == 0:
        pair_rows = key_value_pairs.reshape(seq_count * shard, -1)
        earlier = [block.reshape(key_value_pairs.shape) for block in share_keys(pair_rows)]
    else:
        earlier = []
        for hop in range(1, preds + 1):
            earlier.append(from_behind(key_value_pairs, "ctx", hop))
    results = []
    for seq in range(seq_count):
        window = [block[seq] for block in earlier[::-1]] + [key_value_pairs[seq]]
        results.append(attend(query_rows[seq], grad_attn[seq], window))
    attended, grad_query, *pieces = (jnp.stack(parts) for parts in zip(*results))
    layer_out = jnp.einsum("sic,dc->sid", attended, full_out, preferred_element_type=jnp.float32)
    x_prev = (x_next.astype(jnp.float32) - 2.0 * layer_out).astype(jnp.bfloat16)
    hidden_rows = hidden.reshape(seq_count * shard, width)
    cot_rows = cot_next.reshape(seq_count * shard, width)
    query_left = grad_query.reshape(seq_count * shard, -1)
    attended_rows = attended.reshape(seq_count * shard, -1)
    contract_rows = (((0,), (0,)), ((), ()))
    ctx_count = lax.axis_size("ctx")
    fsdp_count = lax.axis_size("fsdp")
    term_q = lax.dot_general(
        hidden_rows, query_left, contract_rows, preferred_element_type=jnp.float32
    )
    term_out = 2.0 * lax.dot_general(
        cot_rows, attended_rows, contract_rows, preferred_element_type=jnp.float32
    )
    token_total = seq_count * shard * ctx_count * fsdp_count
    grad_weights, grad_kv = reduce_terms(
        term_q.astype(jnp.bfloat16),
        term_out.astype(jnp.bfloat16),
        hidden_rows,
        [piece.reshape(seq_count * shard, -1) for piece in pieces],
        1.0 / math.sqrt(token_total),
    )
    grad_kv = grad_kv.reshape(seq_count, shard, -1)
    grad_hidden = jnp.einsum("sic,dc->sid", grad_query, full_q, preferred_element_type=jnp.float32)
    grad_hidden = grad_hidden + jnp.einsum(
        "sic,dc->sid", grad_kv, full_kv, preferred_element_type=jnp.float32
    )
    grad_x = inv_rms * (
        grad_hidden - normed * jnp.mean(grad_hidden * normed, axis=-1, keepdims=True)
    )
    grad_cur = (cot_cur.astype(jnp.float32) + grad_x).astype(jnp.bfloat16)
    return (x_prev, grad_cur, grad_weights)


def solution(mesh):
    in_specs = (
        P("fsdp", "ctx", None),
        P("fsdp", "ctx", None),
        P("fsdp", "ctx", None),
        P("fsdp", "ctx", None),
        P("fsdp", None),
        P("fsdp", None),
        P("fsdp", None),
    )
    out_specs = (P("fsdp", "ctx", None), P("fsdp", "ctx", None), P(("ctx", "fsdp"), None))
    return jax.shard_map(shards, mesh=mesh, in_specs=in_specs, out_specs=out_specs, check_vma=False)
```
